768 devices in a mesh: ctx: 96 (over x, z, core), head: 8 (over y).
Axes of the slice: x: 4, y: 8, z: 12, core: 2. Of those that a mesh axis runs over, the one named last changes fastest.
Arguments:
- query_all_heads: bfloat16 [24576, 8192], P('ctx', 'head'), may hold values from -48 to 48
- key_heads: bfloat16 [24576, 1024], P('ctx', 'head'), may hold values from -20 to 20
- value_all_heads: bfloat16 [24576, 1024], P('ctx', 'head'), may hold values from -6 to 6
- attention_output: bfloat16 [24576, 8192], P('ctx', 'head'), may hold values from -3 to 3
- output_gradient: bfloat16 [24576, 8192], P('ctx', 'head'), may hold values from -6 to 6
- key_projection: bfloat16 [8192, 1024], P(None, 'head'), may hold values from -0.1875 to 0.1875
- value_projection: bfloat16 [8192, 1024], P(None, 'head'), may hold values from -0.1875 to 0.1875
- doc_lengths: int32 [96], replicated, may hold values from 1 to 1024, as said below
Outputs:
- grad_queries: bfloat16 [24576, 8192], P('ctx', 'head')
- grad_inputs: bfloat16 [8192, 24576], P('head', 'ctx')
The draws below stay inside these ranges and needn't reach their ends.
Inputs may be any that keep to these rules, and one draw needn't show every extreme that they name: `doc_lengths`: the 96 documents fill the 24576 rows; the longest has exactly 1024 rows.
All inputs are finite; a program needn't handle non-finite values.
Results may differ from the reference program's by a relative error of at most 0.023.
Values may be sent and summed in bfloat16 or wider, within the bound.
A program may use at most 64 MiB of HBM per device.

```python
import jax
import jax.numpy as jnp
from jax import lax

MODEL_WIDTH = 8192
QUERY_HEADS = 64
KEY_VALUE_HEADS = 8
HEAD_SIZE = 128
BLOCK_ROWS = 128
T_DEV = 256
PACKED_TOKENS = 24576
LONGEST_ROWS = 1024
NDOCS = 96
N_HEAD = 8


def doc_first_rows(lengths, row_ids):
    doc_ends = jnp.cumsum(lengths)
    starts = doc_ends - lengths
    inside = starts[None, :] <= row_ids[:, None]
    return jnp.max(jnp.where(inside, starts[None, :], 0), axis=1)


def shared_lengths(key):
    key = jax.random.fold_in(key, 11)
    group_count = NDOCS // 4
    common = jnp.sort(jax.random.randint(jax.random.fold_in(key, 1), (group_count, 3), 0, LONGEST_ROWS - 3), axis=1)
    short_cuts = jnp.sort(jax.random.randint(jax.random.fold_in(key, 2), (3,), 0, LONGEST_ROWS - 6))
    doc_parts = jnp.stack([common[:, 0] + 1, common[:, 1] - common[:, 0] + 1, common[:, 2] - common[:, 1] + 1, LONGEST_ROWS - 3 - common[:, 2]], axis=1)
    shorter = jnp.stack([short_cuts[0] + 1, short_cuts[1] - short_cuts[0] + 1, short_cuts[2] - short_cuts[1] + 1, LONGEST_ROWS - 6 - short_cuts[2]])
    longest = jnp.array([LONGEST_ROWS, 1, 1, 1], jnp.int32)
    doc_parts = doc_parts.astype(jnp.int32).at[0].set(longest).at[1].set(shorter.astype(jnp.int32))
    all_lengths = doc_parts.reshape(NDOCS)
    shuffle = jax.random.permutation(jax.random.fold_in(key, 3), NDOCS)
    return all_lengths[shuffle].astype(jnp.int32)


def shared_keys(key):
    lengths = shared_lengths(key)
    row_ids = jnp.arange(PACKED_TOKENS, dtype=jnp.int32)
    chosen = (row_ids % 61 == 29) & (doc_first_rows(lengths, row_ids) < row_ids)
    base_random_key = jax.random.normal(jax.random.fold_in(key, 23), (PACKED_TOKENS, KEY_VALUE_HEADS * HEAD_SIZE), jnp.float32)
    lifted = jnp.where(chosen[:, None], base_random_key, base_random_key)
    key_random_seed = lifted
    return key_random_seed


def draw_doc_lengths(key, part):
    return shared_lengths(key)


def draw_key_heads(key, part):
    key_random_seed = shared_keys(key)
    return key_random_seed.astype(jnp.bfloat16)


def draw_query_all_heads(key, part):
    own_key = jax.random.fold_in(key, 41)
    return jax.random.normal(own_key, (PACKED_TOKENS, QUERY_HEADS * HEAD_SIZE), jnp.float32).astype(jnp.bfloat16)


def block_levels(stream_key, shape, cuts, smallest, top_value):
    gain, own = 1.0, jax.random.fold_in(stream_key, 6)
    for dim, parts in cuts:
        heights = jnp.exp(jax.random.uniform(jax.random.fold_in(own, dim), (parts,), jnp.float32, smallest / len(cuts), top_value / len(cuts)))
        gain = gain * jnp.repeat(heights, shape[dim] // parts).reshape([-1 if axis == dim else 1 for axis in range(len(shape))])
    return gain


def bell_draw(key, dims, spread, reach, split=(), held_as=jnp.bfloat16):
    result = spread * jax.random.normal(key, dims, jnp.float32)
    if split:
        result = result * block_levels(key, dims, split, -0.22, 0.18)
    return jnp.clip(result, -reach, reach).astype(held_as)


def setup_inputs(seed: int = 0) -> dict:
    streams_of = jax.random.split(jax.random.key(seed), 9)
    query_all_heads = draw_query_all_heads(jax.random.fold_in(streams_of[8], 71), 0)
    key_heads = draw_key_heads(jax.random.fold_in(streams_of[8], 71), 0)
    value_all_heads = bell_draw(streams_of[2], (PACKED_TOKENS, KEY_VALUE_HEADS * HEAD_SIZE), 1.0, 6.0, ((0, 96), (1, 8)))
    attention_output = bell_draw(streams_of[3], (PACKED_TOKENS, QUERY_HEADS * HEAD_SIZE), 0.5, 3.0, ((0, 96), (1, 8)))
    output_gradient = bell_draw(streams_of[4], (PACKED_TOKENS, QUERY_HEADS * HEAD_SIZE), 1.0, 6.0, ((0, 96), (1, 8)))
    key_projection = bell_draw(streams_of[5], (MODEL_WIDTH, KEY_VALUE_HEADS * HEAD_SIZE), (KEY_VALUE_HEADS * HEAD_SIZE) ** -0.5, 0.1875, ((1, 8),))
    value_projection = bell_draw(streams_of[6], (MODEL_WIDTH, KEY_VALUE_HEADS * HEAD_SIZE), (KEY_VALUE_HEADS * HEAD_SIZE) ** -0.5, 0.1875, ((1, 8),))
    doc_lengths = draw_doc_lengths(jax.random.fold_in(streams_of[8], 71), 0)
    return dict(query_all_heads=query_all_heads, key_heads=key_heads, value_all_heads=value_all_heads, attention_output=attention_output, output_gradient=output_gradient, key_projection=key_projection, value_projection=value_projection, doc_lengths=doc_lengths)


NEG_BIG = -1.0e30


def row_starts(doc_lengths, row_ids):
    doc_ends = jnp.cumsum(doc_lengths).astype(jnp.int32)
    starts = (doc_ends - doc_lengths).astype(jnp.int32)
    inside = starts[None, :] <= row_ids[:, None]
    return jnp.max(jnp.where(inside, starts[None, :], 0), axis=1).astype(jnp.int32)


def reference(query_all_heads, key_heads, value_all_heads, attention_output, output_gradient, key_projection, value_projection, doc_lengths):
    heads_per_group = QUERY_HEADS // KEY_VALUE_HEADS
    key_value_width = KEY_VALUE_HEADS * HEAD_SIZE
    score_scale = HEAD_SIZE ** -0.5
    front_pad = LONGEST_ROWS - BLOCK_ROWS
    padded_key_rows = jnp.concatenate([jnp.zeros((front_pad, key_value_width), key_heads.dtype), key_heads], axis=0)
    padded_value_rows = jnp.concatenate([jnp.zeros((front_pad, key_value_width), value_all_heads.dtype), value_all_heads], axis=0)
    block_total = PACKED_TOKENS // BLOCK_ROWS

    def block_step(carried, block_index):
        key_acc, value_acc = carried
        leading_row = block_index * BLOCK_ROWS
        query_by_head = lax.dynamic_slice_in_dim(query_all_heads, leading_row, BLOCK_ROWS, 0).astype(jnp.float32).reshape(BLOCK_ROWS, KEY_VALUE_HEADS, heads_per_group, HEAD_SIZE)
        gradient_by_head = lax.dynamic_slice_in_dim(output_gradient, leading_row, BLOCK_ROWS, 0).astype(jnp.float32).reshape(BLOCK_ROWS, KEY_VALUE_HEADS, heads_per_group, HEAD_SIZE)
        output_by_head = lax.dynamic_slice_in_dim(attention_output, leading_row, BLOCK_ROWS, 0).astype(jnp.float32).reshape(BLOCK_ROWS, KEY_VALUE_HEADS, heads_per_group, HEAD_SIZE)
        key_by_head = lax.dynamic_slice_in_dim(padded_key_rows, leading_row, LONGEST_ROWS, 0).astype(jnp.float32).reshape(LONGEST_ROWS, KEY_VALUE_HEADS, HEAD_SIZE)
        value_by_head = lax.dynamic_slice_in_dim(padded_value_rows, leading_row, LONGEST_ROWS, 0).astype(jnp.float32).reshape(LONGEST_ROWS, KEY_VALUE_HEADS, HEAD_SIZE)
        query_rows = leading_row + jnp.arange(BLOCK_ROWS, dtype=jnp.int32)
        key_rows = leading_row - front_pad + jnp.arange(LONGEST_ROWS, dtype=jnp.int32)
        query_start = row_starts(doc_lengths, query_rows)
        visible = (key_rows[None, :] <= query_rows[:, None]) & (key_rows[None, :] >= query_start[:, None])
        scores = jnp.einsum("qkgd,tkd->kgqt", query_by_head, key_by_head) * score_scale
        masked = jnp.where(visible, scores, NEG_BIG)
        row_max = jnp.max(masked, axis=-1, keepdims=True)
        row_total = jnp.sum(jnp.where(visible, jnp.exp(masked - row_max), 0.0), axis=-1, keepdims=True)
        log_total = row_max + jnp.log(row_total)
        softmax_w = jnp.where(visible, jnp.exp(masked - log_total), 0.0)
        rounded_w = lax.optimization_barrier(softmax_w.astype(jnp.bfloat16)).astype(jnp.float32)
        out_dot = jnp.einsum("qkgd,qkgd->kgq", gradient_by_head, output_by_head)[..., None]
        grad_probs = jnp.einsum("qkgd,tkd->kgqt", gradient_by_head, value_by_head)
        grad_scores = softmax_w * (grad_probs - out_dot)
        grad_rounded = lax.optimization_barrier(grad_scores.astype(jnp.bfloat16)).astype(jnp.float32)
        query_grad = jnp.einsum("kgqt,tkd->qkgd", grad_rounded, key_by_head) * score_scale
        key_grad = jnp.einsum("kgqt,qkgd->tkd", grad_rounded, query_by_head) * score_scale
        value_grad = jnp.einsum("kgqt,qkgd->tkd", rounded_w, gradient_by_head)
        old_keys = lax.dynamic_slice_in_dim(key_acc, leading_row, LONGEST_ROWS, 0)
        key_acc = lax.dynamic_update_slice_in_dim(key_acc, old_keys + key_grad.reshape(LONGEST_ROWS, key_value_width), leading_row, 0)
        old_values = lax.dynamic_slice_in_dim(value_acc, leading_row, LONGEST_ROWS, 0)
        value_acc = lax.dynamic_update_slice_in_dim(value_acc, old_values + value_grad.reshape(LONGEST_ROWS, key_value_width), leading_row, 0)
        return (key_acc, value_acc), query_grad.reshape(BLOCK_ROWS, QUERY_HEADS * HEAD_SIZE).astype(jnp.bfloat16)

    start_acc = jnp.zeros((front_pad + PACKED_TOKENS, key_value_width), jnp.float32)
    (key_acc, value_acc), query_blocks = lax.scan(block_step, (start_acc, start_acc), jnp.arange(block_total, dtype=jnp.int32))
    grad_queries = query_blocks.reshape(PACKED_TOKENS, QUERY_HEADS * HEAD_SIZE)
    key_grads = key_acc[front_pad:].astype(jnp.bfloat16)
    value_grads = value_acc[front_pad:].astype(jnp.bfloat16)
    heads_per_device = KEY_VALUE_HEADS // N_HEAD
    key_weights = key_projection.astype(jnp.float32).reshape(MODEL_WIDTH, N_HEAD, heads_per_device * HEAD_SIZE)
    value_weights = value_projection.astype(jnp.float32).reshape(MODEL_WIDTH, N_HEAD, heads_per_device * HEAD_SIZE)

    def token_block(block_index):
        key_part = lax.dynamic_slice_in_dim(key_grads, block_index * T_DEV, T_DEV, 0).astype(jnp.float32).reshape(T_DEV, N_HEAD, heads_per_device * HEAD_SIZE)
        value_part = lax.dynamic_slice_in_dim(value_grads, block_index * T_DEV, T_DEV, 0).astype(jnp.float32).reshape(T_DEV, N_HEAD, heads_per_device * HEAD_SIZE)
        partial_value = jnp.einsum("dhw,thw->hdt", key_weights, key_part) + jnp.einsum("dhw,thw->hdt", value_weights, value_part)
        partial_value = lax.optimization_barrier(partial_value.astype(jnp.bfloat16)).astype(jnp.float32)
        return jnp.sum(partial_value, axis=0).astype(jnp.bfloat16)

    pieces = lax.map(token_block, jnp.arange(PACKED_TOKENS // T_DEV, dtype=jnp.int32))
    grad_inputs = jnp.transpose(pieces, (1, 0, 2)).reshape(MODEL_WIDTH, PACKED_TOKENS)
    return grad_queries, grad_inputs
```

```python
import functools

import jax
import jax.numpy as jnp
from jax import lax
from jax.experimental import pallas as pl
from jax.experimental.pallas import tpu as pltpu
from jax.sharding import PartitionSpec as P

MESH = pl.DeviceIdType.MESH
HEAD_SIZE = 128
BLOCK_ROWS = 128
LONGEST_ROWS = 1024
X_CHIPS = 4
NEG_BIG = -1.0e30
LOG2E = 1.4426950408889634

F32 = jnp.float32
BF16 = jnp.bfloat16


def dot_nn(a, b):
    return lax.dot_general(a, b, (((1,), (0,)), ((), ())), preferred_element_type=F32)


def dot_nt(a, b):
    return lax.dot_general(a, b, (((1,), (1,)), ((), ())), preferred_element_type=F32)


def kernel(
    n_ctx, n_y, n_x,
    q_hbm, k_hbm, v_hbm, o_hbm, g_hbm, kp_hbm, vp_hbm, doc_ref,
    dq_hbm, gi_hbm,
    q_ref, g_ref, o_ref, qt_ref, gt_ref, kwin, vwin, bias_ref, p_ref, ds_ref,
    w_ref, all_ref, term_ref, inbox_ref, own_ref, acc_ref, dq_ref, gi_ref,
    load_sem, out_sem, ctx_send, ctx_recv, term_send, term_recv,
    wy_send, wy_recv, wx_send, wx_recv, wc_send, wc_recv, ay_send, ay_recv,
):
    rows, width = q_hbm.shape
    heads = width // HEAD_SIZE
    back = LONGEST_ROWS - BLOCK_ROWS
    win = back + rows
    reach = LONGEST_ROWS // rows
    model_rows = gi_hbm.shape[0]
    part_rows = model_rows // (2 * n_x)
    scale = HEAD_SIZE ** -0.5

    c = lax.axis_index("ctx")
    y = lax.axis_index("head")
    per_x = n_ctx // n_x
    x = c // per_x
    inner = c % per_x
    core = c % 2
    peer = c + 1 - 2 * core

    def at_ctx(i):
        return (lax.rem(c + i + n_ctx, n_ctx), y)

    def at_y(i):
        return (c, lax.rem(y + i + n_y, n_y))

    def at_x(i):
        return (lax.rem(x + i, n_x) * per_x + inner, y)

    def remote(src, dst, send, recv, to):
        return pltpu.make_async_remote_copy(
            src_ref=src, dst_ref=dst, send_sem=send, recv_sem=recv, device_id=to, device_id_type=MESH
        )

    loads = [
        pltpu.make_async_copy(k_hbm, kwin.at[pl.ds(back, rows), :], load_sem.at[0]),
        pltpu.make_async_copy(v_hbm, vwin.at[pl.ds(back, rows), :], load_sem.at[1]),
        pltpu.make_async_copy(q_hbm, q_ref, load_sem.at[2]),
        pltpu.make_async_copy(g_hbm, g_ref, load_sem.at[3]),
        pltpu.make_async_copy(o_hbm, o_ref, load_sem.at[4]),
    ]
    my_part = pl.multiple_of((x * 2 + core) * part_rows, part_rows)
    my_rows = pl.multiple_of(y * model_rows + my_part, part_rows)
    for kv, src in ((0, kp_hbm), (1, vp_hbm)):
        loads.append(pltpu.make_async_copy(
            src.at[pl.ds(my_rows, part_rows), :],
            w_ref.at[kv * n_y + y, pl.ds(my_part, part_rows), :],
            load_sem.at[5 + kv],
        ))
    for copy in loads:
        copy.start()

    barrier = pltpu.get_barrier_semaphore()
    partners = [at_ctx(i) for i in range(-reach, reach + 1) if i != 0]
    partners += [at_y(i) for i in range(1, n_y)] + [at_x(i) for i in range(1, n_x)]
    for to in partners:
        pl.semaphore_signal(barrier, inc=1, device_id=to, device_id_type=MESH)
    pl.semaphore_wait(barrier, len(partners))

    def context_copies(kv, src, dst):
        copies = []
        for i in range(1, reach + 1):
            first = max(back - i * rows, 0)
            cut = max(i * rows - back, 0)
            copies.append(remote(
                src.at[pl.ds(cut, rows - cut), :], dst.at[pl.ds(first, rows - cut), :],
                ctx_send.at[kv * reach + i - 1], ctx_recv.at[kv * reach + i - 1], at_ctx(i),
            ))
        return copies

    key_copies = context_copies(0, k_hbm, kwin)
    value_copies = context_copies(1, v_hbm, vwin)
    for copy in key_copies:
        copy.start()

    wy_copies = []
    for i in range(1, n_y):
        other = lax.rem(y + i, n_y)
        theirs = pl.multiple_of(other * model_rows + my_part, part_rows)
        for kv, src in ((0, kp_hbm), (1, vp_hbm)):
            wy_copies.append(remote(
                src.at[pl.ds(theirs, part_rows), :],
                w_ref.at[kv * n_y + y, pl.ds(my_part, part_rows), :],
                wy_send.at[2 * (i - 1) + kv], wy_recv.at[2 * (i - 1) + kv], at_y(i),
            ))
    for copy in wy_copies:
        copy.start()

    docs = doc_ref.shape[1]
    lens = jnp.broadcast_to(doc_ref[...].astype(F32), (docs, docs))
    sub = lax.broadcasted_iota(jnp.int32, (docs, docs), 0)
    lane = lax.broadcasted_iota(jnp.int32, (docs, docs), 1)
    lens_col = jnp.sum(jnp.where(sub == lane, lens, 0.0), axis=1, keepdims=True)
    starts = jnp.sum(jnp.where(sub < lane, lens_col, 0.0), axis=0, keepdims=True)
    row_abs = (lax.broadcasted_iota(jnp.int32, (rows, docs), 0) + c * rows).astype(F32)
    row_start = jnp.max(jnp.where(starts <= row_abs, starts, 0.0), axis=1, keepdims=True)
    row_id = lax.broadcasted_iota(jnp.int32, (rows, 1), 0)
    low = row_start - (row_id + c * rows).astype(F32) + row_id.astype(F32)
    low = jnp.maximum(low, ((row_id // BLOCK_ROWS) * BLOCK_ROWS - back).astype(F32))
    for first in range(0, win, 128):
        key_rel = (lax.broadcasted_iota(jnp.int32, (rows, 128), 1) + (first - back)).astype(F32)
        seen = (key_rel <= row_id.astype(F32)) & (key_rel >= low)
        bias_ref[:, first:first + 128] = jnp.where(seen, 0.0, NEG_BIG)

    loads[2].wait()
    loads[3].wait()
    for h in range(heads):
        cols = slice(h * HEAD_SIZE, (h + 1) * HEAD_SIZE)
        qt_ref[:, h * rows:(h + 1) * rows] = q_ref[:, cols].T
        gt_ref[:, h * rows:(h + 1) * rows] = g_ref[:, cols].T

    loads[0].wait()
    for copy in key_copies:
        copy.wait_recv()
    for copy in value_copies:
        copy.start()

    def head_cols(h):
        return pl.ds(pl.multiple_of(h * HEAD_SIZE, HEAD_SIZE), HEAD_SIZE)

    def head_rows(h):
        return pl.ds(pl.multiple_of(h * rows, rows), rows)

    def softmax_head(h, _):
        s = dot_nt(q_ref[:, head_cols(h)], kwin[...]) * (scale * LOG2E) + bias_ref[...]
        top = jnp.max(s, axis=1, keepdims=True)
        e = jnp.exp2(s - top)
        total = jnp.sum(e, axis=1, keepdims=True)
        p_ref[head_rows(h), :] = (e * (1.0 / total)).astype(BF16)
        return 0

    lax.fori_loop(0, heads, softmax_head, 0)

    chunks = [(0, rows - (reach * rows - back), reach)]
    chunks += [(back - i * rows, rows, i) for i in range(reach - 1, -1, -1)]

    def term_copies(kv):
        copies = []
        for first, size, i in chunks[:-1]:
            copies.append(remote(
                term_ref.at[kv, i - 1, :, pl.ds(rows - size, size)],
                inbox_ref.at[kv, i - 1, :, pl.ds(rows - size, size)],
                term_send.at[kv * reach + i - 1], term_recv.at[kv * reach + i - 1], at_ctx(-i),
            ))
        return copies

    def terms(kv, left_ref, right_ref, factor):
        copies = term_copies(kv)
        for (first, size, i), copy in zip(chunks, copies + [None]):
            part = dot_nn(left_ref[...], right_ref[:, first:first + size])
            if factor != 1.0:
                part = part * factor
            if i > 0:
                term_ref[kv, i - 1, :, rows - size:] = part.astype(BF16)
                copy.start()
            else:
                own_ref[kv] = part
        return copies

    value_terms = terms(1, gt_ref, p_ref, 1.0)

    loads[5].wait()
    loads[6].wait()
    for copy in wy_copies:
        copy.wait_recv()
    wx_copies = []
    mine = w_ref.at[:, pl.ds(my_part, part_rows), :]
    for i in range(1, n_x):
        wx_copies.append(remote(mine, mine, wx_send.at[i - 1], wx_recv.at[i - 1], at_x(i)))
    for copy in wx_copies:
        copy.start()
    wc_copies = []
    for i in range(n_x):
        came = lax.rem(x - i + n_x, n_x)
        part = w_ref.at[:, pl.ds(pl.multiple_of((came * 2 + core) * part_rows, part_rows), part_rows), :]
        wc_copies.append(remote(part, part, wc_send.at[i], wc_recv.at[i], (peer, y)))
    wc_copies[0].start()

    loads[1].wait()
    loads[4].wait()
    for copy in value_copies:
        copy.wait_recv()

    def score_head(h, _):
        grad = g_ref[:, head_cols(h)]
        delta = jnp.sum(grad.astype(F32) * o_ref[:, head_cols(h)].astype(F32), axis=1, keepdims=True)
        dp = dot_nt(grad, vwin[...])
        ds_ref[head_rows(h), :] = (p_ref[head_rows(h), :].astype(F32) * (dp - delta)).astype(BF16)
        return 0

    def query_head(h, _):
        dq = dot_nn(ds_ref[head_rows(h), :], kwin[...]) * scale
        dq_ref[:, head_cols(h)] = dq.astype(BF16)
        return 0

    def own_sum(kv, copies):
        for copy in copies:
            copy.wait_recv()
        total = own_ref[kv]
        for i in range(1, reach):
            total = total + inbox_ref[kv, i - 1].astype(F32)
        size = chunks[0][1]
        cut = rows - size
        last = total[:, cut:] + inbox_ref[kv, reach - 1, :, cut:].astype(F32)
        slab = kv * n_y + y
        all_ref[slab, :, :cut] = total[:, :cut].astype(BF16)
        all_ref[slab, :, cut:] = last.astype(BF16)

    n_up = n_y // 2
    n_down = (n_y - 1) // 2

    def gather_step(kv, s):
        copies = []
        if s < n_up:
            slab = all_ref.at[kv * n_y + lax.rem(y - s + n_y, n_y)]
            k = kv * (n_up + n_down) + s
            copies.append(remote(slab, slab, ay_send.at[k], ay_recv.at[k], at_y(1)))
        if s < n_down:
            slab = all_ref.at[kv * n_y + lax.rem(y + s, n_y)]
            k = kv * (n_up + n_down) + n_up + s
            copies.append(remote(slab, slab, ay_send.at[k], ay_recv.at[k], at_y(-1)))
        return copies

    gathered = []

    def start_gather(kv, s):
        copies = gather_step(kv, s)
        for copy in copies:
            copy.start()
        gathered.append(copies)

    def wait_gather():
        for copy in gathered[-1]:
            copy.wait_recv()

    per = max(heads // 4, 1)
    lax.fori_loop(0, per, score_head, 0)
    own_sum(1, value_terms)
    start_gather(1, 0)
    for s in range(1, 4):
        lax.fori_loop(s * per, (s + 1) * per, score_head, 0)
        if s < n_up:
            wait_gather()
            start_gather(1, s)

    key_terms = terms(0, qt_ref, ds_ref, scale)
    lax.fori_loop(0, heads // 2, query_head, 0)
    for i in range(1, n_x):
        wx_copies[i - 1].wait_recv()
        wc_copies[i].start()
    own_sum(0, key_terms)
    wait_gather()
    start_gather(0, 0)
    lax.fori_loop(heads // 2, heads, query_head, 0)
    dq_out = pltpu.make_async_copy(dq_ref, dq_hbm, out_sem.at[0])
    dq_out.start()
    for copy in wc_copies:
        copy.wait_recv()

    tile = 256
    tiles = model_rows // tile

    def project(kv, t):
        row = pl.ds(pl.multiple_of(t * tile, tile), tile)
        left = jnp.concatenate([w_ref[kv * n_y + g, row, :] for g in range(n_y)], axis=1)
        right = all_ref[kv * n_y:(kv + 1) * n_y].reshape(n_y * HEAD_SIZE, rows)
        return row, dot_nn(left, right)

    def project_values(t, _):
        row, part = project(1, t)
        acc_ref[row, :] = part
        return 0

    def project_keys(t, _):
        row, part = project(0, t)
        gi_ref[row, :] = (acc_ref[row, :] + part).astype(BF16)
        return 0

    steps = list(range(1, max(n_up, 1)))
    lax.fori_loop(0, tiles // 2, project_values, 0)
    for s in steps[:1]:
        wait_gather()
        start_gather(0, s)
    lax.fori_loop(tiles // 2, tiles, project_values, 0)
    for s in steps[1:]:
        wait_gather()
        start_gather(0, s)
    wait_gather()
    lax.fori_loop(0, tiles, project_keys, 0)
    gi_out = pltpu.make_async_copy(gi_ref, gi_hbm, out_sem.at[1])
    gi_out.start()

    for copy in key_copies + value_copies + wy_copies + wx_copies + wc_copies + value_terms + key_terms:
        copy.wait_send()
    for copies in gathered:
        for copy in copies:
            copy.wait_send()
    dq_out.wait()
    gi_out.wait()


def body(n_ctx, n_y, n_x, q, k, v, o, g, kp, vp, doc_lengths):
    rows, width = q.shape
    heads = width // HEAD_SIZE
    model_rows = kp.shape[0] // n_y
    reach = LONGEST_ROWS // rows
    win = LONGEST_ROWS - BLOCK_ROWS + rows
    hops = n_y - 1
    dma = pltpu.SemaphoreType.DMA
    any_spec = pl.BlockSpec(memory_space=pl.ANY)
    return pl.pallas_call(
        functools.partial(kernel, n_ctx, n_y, n_x),
        out_shape=(
            jax.ShapeDtypeStruct((rows, width), BF16),
            jax.ShapeDtypeStruct((model_rows, rows), BF16),
        ),
        in_specs=[any_spec] * 7 + [pl.BlockSpec(memory_space=pltpu.VMEM)],
        out_specs=(any_spec, any_spec),
        scratch_shapes=[
            pltpu.VMEM((rows, width), BF16),
            pltpu.VMEM((rows, width), BF16),
            pltpu.VMEM((rows, width), BF16),
            pltpu.VMEM((HEAD_SIZE, heads * rows), BF16),
            pltpu.VMEM((HEAD_SIZE, heads * rows), BF16),
            pltpu.VMEM((win, HEAD_SIZE), BF16),
            pltpu.VMEM((win, HEAD_SIZE), BF16),
            pltpu.VMEM((rows, win), F32),
            pltpu.VMEM((heads * rows, win), BF16),
            pltpu.VMEM((heads * rows, win), BF16),
            pltpu.VMEM((2 * n_y, model_rows, HEAD_SIZE), BF16),
            pltpu.VMEM((2 * n_y, HEAD_SIZE, rows), BF16),
            pltpu.VMEM((2, reach, HEAD_SIZE, rows), BF16),
            pltpu.VMEM((2, reach, HEAD_SIZE, rows), BF16),
            pltpu.VMEM((2, HEAD_SIZE, rows), F32),
            pltpu.VMEM((model_rows, rows), F32),
            pltpu.VMEM((rows, width), BF16),
            pltpu.VMEM((model_rows, rows), BF16),
            dma((7,)), dma((2,)),
            dma((2 * reach,)), dma((2 * reach,)),
            dma((2 * reach,)), dma((2 * reach,)),
            dma((2 * hops,)), dma((2 * hops,)),
            dma((n_x - 1,)), dma((n_x - 1,)),
            dma((n_x,)), dma((n_x,)),
            dma((2 * hops,)), dma((2 * hops,)),
        ],
        compiler_params=pltpu.CompilerParams(
            collective_id=0, has_side_effects=True, vmem_limit_bytes=56 * 1024 * 1024
        ),
    )(q, k, v, o, g, kp, vp, doc_lengths.reshape(1, -1))


def build(mesh, n_x):
    return jax.shard_map(
        functools.partial(body, mesh.shape["ctx"], mesh.shape["head"], n_x),
        mesh=mesh,
        in_specs=(
            P("ctx", "head"),
            P("ctx", "head"),
            P("ctx", "head"),
            P("ctx", "head"),
            P("ctx", "head"),
            P(None, "head"),
            P(None, "head"),
            P(),
        ),
        out_specs=(P("ctx", "head"), P("head", "ctx")),
        check_vma=False,
    )


def solution(mesh):
    return build(mesh, X_CHIPS)
```

```python
import functools

import jax
import jax.numpy as jnp
from jax import lax
from jax.experimental import pallas as pl
from jax.experimental.pallas import tpu as pltpu
from jax.sharding import PartitionSpec as P

MESH = pl.DeviceIdType.MESH
HEAD_SIZE = 128
BLOCK_ROWS = 128
LONGEST_ROWS = 1024
X_CHIPS = 4
NEG_BIG = -1.0e30
LOG2E = 1.4426950408889634

F32 = jnp.float32
BF16 = jnp.bfloat16


def dot_nn(a, b):
    return lax.dot_general(a, b, (((1,), (0,)), ((), ())), preferred_element_type=F32)


def dot_nt(a, b):
    return lax.dot_general(a, b, (((1,), (1,)), ((), ())), preferred_element_type=F32)


def kernel(
    n_ctx, n_y, n_x,
    q_hbm, k_hbm, v_hbm, o_hbm, g_hbm, kp_hbm, vp_hbm, doc_ref,
    dq_hbm, gi_hbm,
    q_ref, g_ref, o_ref, qt_ref, gt_ref, kwin, vwin, bias_ref, p_ref, ds_ref,
    w_ref, all_ref, term_ref, inbox_ref, own_ref, acc_ref, dq_ref, gi_ref,
    load_sem, out_sem, ctx_send, ctx_recv, term_send, term_recv,
    wy_send, wy_recv, wx_send, wx_recv, wc_send, wc_recv, ay_send, ay_recv,
):
    rows, width = q_hbm.shape
    heads = width // HEAD_SIZE
    back = LONGEST_ROWS - BLOCK_ROWS
    win = back + rows
    reach = LONGEST_ROWS // rows
    model_rows = gi_hbm.shape[0]
    part_rows = model_rows // (2 * n_x)
    scale = HEAD_SIZE ** -0.5

    c = lax.axis_index("ctx")
    y = lax.axis_index("head")
    per_x = n_ctx // n_x
    x = c // per_x
    inner = c % per_x
    core = c % 2
    peer = c + 1 - 2 * core

    def at_ctx(i):
        return (lax.rem(c + i + n_ctx, n_ctx), y)

    def at_y(i):
        return (c, lax.rem(y + i + n_y, n_y))

    def at_x(i):
        return (lax.rem(x + i, n_x) * per_x + inner, y)

    def remote(src, dst, send, recv, to):
        return pltpu.make_async_remote_copy(
            src_ref=src, dst_ref=dst, send_sem=send, recv_sem=recv, device_id=to, device_id_type=MESH
        )

    loads = [
        pltpu.make_async_copy(k_hbm, kwin.at[pl.ds(back, rows), :], load_sem.at[0]),
        pltpu.make_async_copy(v_hbm, vwin.at[pl.ds(back, rows), :], load_sem.at[1]),
        pltpu.make_async_copy(q_hbm, q_ref, load_sem.at[2]),
        pltpu.make_async_copy(g_hbm, g_ref, load_sem.at[3]),
        pltpu.make_async_copy(o_hbm, o_ref, load_sem.at[4]),
    ]
    my_part = pl.multiple_of((x * 2 + core) * part_rows, part_rows)
    my_rows = pl.multiple_of(y * model_rows + my_part, part_rows)
    for kv, src in ((0, kp_hbm), (1, vp_hbm)):
        loads.append(pltpu.make_async_copy(
            src.at[pl.ds(my_rows, part_rows), :],
            w_ref.at[kv * n_y + y, pl.ds(my_part, part_rows), :],
            load_sem.at[5 + kv],
        ))
    for copy in loads:
        copy.start()

    loads[0].wait()
    loads[1].wait()
    barrier = pltpu.get_barrier_semaphore()
    partners = [at_ctx(i) for i in range(-reach, reach + 1) if i != 0]
    partners += [at_y(i) for i in range(1, n_y)] + [at_x(i) for i in range(1, n_x)]
    for to in partners:
        pl.semaphore_signal(barrier, inc=1, device_id=to, device_id_type=MESH)
    pl.semaphore_wait(barrier, len(partners))

    def context_copies(kv, ref):
        copies = []
        for i in range(1, reach + 1):
            first = max(back - i * rows, 0)
            cut = max(i * rows - back, 0)
            copies.append(remote(
                ref.at[pl.ds(back + cut, rows - cut), :], ref.at[pl.ds(first, rows - cut), :],
                ctx_send.at[kv * reach + i - 1], ctx_recv.at[kv * reach + i - 1], at_ctx(i),
            ))
        return copies

    key_copies = context_copies(0, kwin)
    value_copies = context_copies(1, vwin)
    for copy in key_copies:
        copy.start()

    wy_copies = []
    for i in range(1, n_y):
        other = lax.rem(y + i, n_y)
        theirs = pl.multiple_of(other * model_rows + my_part, part_rows)
        for kv, src in ((0, kp_hbm), (1, vp_hbm)):
            wy_copies.append(remote(
                src.at[pl.ds(theirs, part_rows), :],
                w_ref.at[kv * n_y + y, pl.ds(my_part, part_rows), :],
                wy_send.at[2 * (i - 1) + kv], wy_recv.at[2 * (i - 1) + kv], at_y(i),
            ))
    for copy in wy_copies:
        copy.start()

    docs = doc_ref.shape[1]
    lens = jnp.broadcast_to(doc_ref[...].astype(F32), (docs, docs))
    sub = lax.broadcasted_iota(jnp.int32, (docs, docs), 0)
    lane = lax.broadcasted_iota(jnp.int32, (docs, docs), 1)
    lens_col = jnp.sum(jnp.where(sub == lane, lens, 0.0), axis=1, keepdims=True)
    starts = jnp.sum(jnp.where(sub < lane, lens_col, 0.0), axis=0, keepdims=True)
    row_abs = (lax.broadcasted_iota(jnp.int32, (rows, docs), 0) + c * rows).astype(F32)
    row_start = jnp.max(jnp.where(starts <= row_abs, starts, 0.0), axis=1, keepdims=True)
    row_id = lax.broadcasted_iota(jnp.int32, (rows, 1), 0)
    low = row_start - (row_id + c * rows).astype(F32) + row_id.astype(F32)
    low = jnp.maximum(low, ((row_id // BLOCK_ROWS) * BLOCK_ROWS - back).astype(F32))
    for first in range(0, win, 128):
        key_rel = (lax.broadcasted_iota(jnp.int32, (rows, 128), 1) + (first - back)).astype(F32)
        seen = (key_rel <= row_id.astype(F32)) & (key_rel >= low)
        bias_ref[:, first:first + 128] = jnp.where(seen, 0.0, NEG_BIG)

    loads[2].wait()
    loads[3].wait()
    for h in range(heads):
        cols = slice(h * HEAD_SIZE, (h + 1) * HEAD_SIZE)
        qt_ref[:, h * rows:(h + 1) * rows] = q_ref[:, cols].T
        gt_ref[:, h * rows:(h + 1) * rows] = g_ref[:, cols].T

    for copy in key_copies:
        copy.wait_recv()
    for copy in value_copies:
        copy.start()

    def head_cols(h):
        return pl.ds(pl.multiple_of(h * HEAD_SIZE, HEAD_SIZE), HEAD_SIZE)

    def head_rows(h):
        return pl.ds(pl.multiple_of(h * rows, rows), rows)

    def softmax_head(h, _):
        s = dot_nt(q_ref[:, head_cols(h)], kwin[...]) * (scale * LOG2E) + bias_ref[...]
        top = jnp.max(s, axis=1, keepdims=True)
        e = jnp.exp2(s - top)
        total = jnp.sum(e, axis=1, keepdims=True)
        p_ref[head_rows(h), :] = (e * (1.0 / total)).astype(BF16)
        return 0

    lax.fori_loop(0, heads, softmax_head, 0)

    chunks = [(0, rows - (reach * rows - back), reach)]
    chunks += [(back - i * rows, rows, i) for i in range(reach - 1, -1, -1)]

    def term_copies(kv):
        copies = []
        for first, size, i in chunks[:-1]:
            copies.append(remote(
                term_ref.at[kv, i - 1, :, pl.ds(rows - size, size)],
                inbox_ref.at[kv, i - 1, :, pl.ds(rows - size, size)],
                term_send.at[kv * reach + i - 1], term_recv.at[kv * reach + i - 1], at_ctx(-i),
            ))
        return copies

    def terms(kv, left_ref, right_ref, factor):
        copies = term_copies(kv)
        for (first, size, i), copy in zip(chunks, copies + [None]):
            part = dot_nn(left_ref[...], right_ref[:, first:first + size])
            if factor != 1.0:
                part = part * factor
            if i > 0:
                term_ref[kv, i - 1, :, rows - size:] = part.astype(BF16)
                copy.start()
            else:
                own_ref[kv] = part
        return copies

    value_terms = terms(1, gt_ref, p_ref, 1.0)

    loads[5].wait()
    loads[6].wait()
    for copy in wy_copies:
        copy.wait_recv()

    def row_part(i):
        first = (lax.rem(x + i + n_x, n_x) * 2 + core) * part_rows
        return pl.ds(pl.multiple_of(first, part_rows), part_rows)

    mine = w_ref.at[:, row_part(0), :]
    before = w_ref.at[pl.ds(0, n_y), row_part(-1), :]
    after = w_ref.at[pl.ds(n_y, n_y), row_part(1), :]
    wx_copies = [
        remote(mine, mine, wx_send.at[0], wx_recv.at[0], at_x(1)),
        remote(mine, mine, wx_send.at[1], wx_recv.at[1], at_x(n_x - 1)),
        remote(before, before, wx_send.at[2], wx_recv.at[2], at_x(1)),
        remote(after, after, wx_send.at[3], wx_recv.at[3], at_x(n_x - 1)),
    ]
    wc_copies = []
    for k, i in enumerate((0, -1, 1, 2)):
        part = w_ref.at[:, row_part(i), :]
        wc_copies.append(remote(part, part, wc_send.at[k], wc_recv.at[k], (peer, y)))
    wx_copies[0].start()
    wx_copies[1].start()
    wc_copies[0].start()

    loads[4].wait()
    for copy in value_copies:
        copy.wait_recv()

    def score_head(h, _):
        grad = g_ref[:, head_cols(h)]
        delta = jnp.sum(grad.astype(F32) * o_ref[:, head_cols(h)].astype(F32), axis=1, keepdims=True)
        dp = dot_nt(grad, vwin[...])
        ds_ref[head_rows(h), :] = (p_ref[head_rows(h), :].astype(F32) * (dp - delta)).astype(BF16)
        return 0

    def query_head(h, _):
        dq = dot_nn(ds_ref[head_rows(h), :], kwin[...]) * scale
        dq_ref[:, head_cols(h)] = dq.astype(BF16)
        return 0

    def own_sum(kv, copies):
        for copy in copies:
            copy.wait_recv()
        total = own_ref[kv]
        for i in range(1, reach):
            total = total + inbox_ref[kv, i - 1].astype(F32)
        size = chunks[0][1]
        cut = rows - size
        last = total[:, cut:] + inbox_ref[kv, reach - 1, :, cut:].astype(F32)
        slab = kv * n_y + y
        all_ref[slab, :, :cut] = total[:, :cut].astype(BF16)
        all_ref[slab, :, cut:] = last.astype(BF16)


    way = 1 - 2 * core

    def slab_at(kv, i):
        return kv * n_y + lax.rem(y + way * i + n_y, n_y)

    def gather_copies(kv):
        copies = []
        for k, (i, j) in enumerate(((0, 2), (0, -2), (0, 1), (0, -1), (-2, 1), (2, -1), (-2, 2))):
            slab = all_ref.at[slab_at(kv, i)]
            copies.append(remote(slab, slab, ay_send.at[kv * 7 + k], ay_recv.at[kv * 7 + k], at_y(way * j)))
        return copies

    def gather_first(copies):
        for copy in copies[:4]:
            copy.start()

    def gather_second(copies):
        copies[0].wait_recv()
        copies[4].start()
        copies[1].wait_recv()
        copies[5].start()
        copies[6].start()

    lax.fori_loop(0, heads, score_head, 0)
    key_terms = terms(0, qt_ref, ds_ref, scale)
    own_sum(1, value_terms)
    value_gather = gather_copies(1)
    gather_first(value_gather)
    wx_copies[0].wait_recv()
    wx_copies[2].start()
    wc_copies[1].start()
    wx_copies[1].wait_recv()
    wx_copies[3].start()
    wc_copies[2].start()
    lax.fori_loop(0, heads // 2, query_head, 0)
    gather_second(value_gather)
    lax.fori_loop(heads // 2, heads, query_head, 0)
    dq_out = pltpu.make_async_copy(dq_ref, dq_hbm, out_sem.at[0])
    dq_out.start()
    own_sum(0, key_terms)
    key_gather = gather_copies(0)
    gather_first(key_gather)
    wx_copies[2].wait_recv()
    wx_copies[3].wait_recv()
    wc_copies[3].start()
    for copy in wc_copies:
        copy.wait_recv()
    for copy in value_gather[2:]:
        copy.wait_recv()

    tile = 256
    tiles = model_rows // tile

    def project(kv, t, slabs):
        row = pl.ds(pl.multiple_of(t * tile, tile), tile)
        left = jnp.concatenate([w_ref[g, row, :] for g in slabs], axis=1)
        right = jnp.concatenate([all_ref[g] for g in slabs], axis=0)
        return row, dot_nn(left, right)

    def project_values(t, _):
        row, part = project(1, t, range(n_y, 2 * n_y))
        acc_ref[row, :] = part
        return 0

    def project_near(t, _):
        row, part = project(0, t, [slab_at(0, i) for i in (-2, 2, 0, -1, 1)])
        acc_ref[row, :] = acc_ref[row, :] + part
        return 0

    def project_far(t, _):
        row, part = project(0, t, [slab_at(0, i) for i in (-3, 3, 4)])
        gi_ref[row, :] = (acc_ref[row, :] + part).astype(BF16)
        return 0

    lax.fori_loop(0, tiles, project_values, 0)
    gather_second(key_gather)
    key_gather[2].wait_recv()
    key_gather[3].wait_recv()
    lax.fori_loop(0, tiles, project_near, 0)
    for copy in key_gather[4:]:
        copy.wait_recv()
    lax.fori_loop(0, tiles, project_far, 0)
    gi_out = pltpu.make_async_copy(gi_ref, gi_hbm, out_sem.at[1])
    gi_out.start()

    for copy in key_copies + value_copies + wy_copies + wx_copies + wc_copies + value_terms + key_terms + value_gather + key_gather:
        copy.wait_send()
    dq_out.wait()
    gi_out.wait()


def hand_over(dq_in, gi_in, dq_out, gi_out, sem):
    copies = [
        pltpu.make_async_copy(dq_in, dq_out, sem.at[0]),
        pltpu.make_async_copy(gi_in, gi_out, sem.at[1]),
    ]
    for copy in copies:
        copy.start()
    for copy in copies:
        copy.wait()


def body(n_ctx, n_y, n_x, q, k, v, o, g, kp, vp, doc_lengths):
    rows, width = q.shape
    heads = width // HEAD_SIZE
    model_rows = kp.shape[0] // n_y
    reach = LONGEST_ROWS // rows
    win = LONGEST_ROWS - BLOCK_ROWS + rows
    hops = n_y - 1
    dma = pltpu.SemaphoreType.DMA
    any_spec = pl.BlockSpec(memory_space=pl.ANY)
    dq, gi = pl.pallas_call(
        functools.partial(kernel, n_ctx, n_y, n_x),
        out_shape=(
            jax.ShapeDtypeStruct((rows, width), BF16),
            jax.ShapeDtypeStruct((model_rows, rows), BF16),
        ),
        in_specs=[any_spec] * 7 + [pl.BlockSpec(memory_space=pltpu.VMEM)],
        out_specs=(any_spec, any_spec),
        scratch_shapes=[
            pltpu.VMEM((rows, width), BF16),
            pltpu.VMEM((rows, width), BF16),
            pltpu.VMEM((rows, width), BF16),
            pltpu.VMEM((HEAD_SIZE, heads * rows), BF16),
            pltpu.VMEM((HEAD_SIZE, heads * rows), BF16),
            pltpu.VMEM((win, HEAD_SIZE), BF16),
            pltpu.VMEM((win, HEAD_SIZE), BF16),
            pltpu.VMEM((rows, win), F32),
            pltpu.VMEM((heads * rows, win), BF16),
            pltpu.VMEM((heads * rows, win), BF16),
            pltpu.VMEM((2 * n_y, model_rows, HEAD_SIZE), BF16),
            pltpu.VMEM((2 * n_y, HEAD_SIZE, rows), BF16),
            pltpu.VMEM((2, reach, HEAD_SIZE, rows), BF16),
            pltpu.VMEM((2, reach, HEAD_SIZE, rows), BF16),
            pltpu.VMEM((2, HEAD_SIZE, rows), F32),
            pltpu.VMEM((model_rows, rows), F32),
            pltpu.VMEM((rows, width), BF16),
            pltpu.VMEM((model_rows, rows), BF16),
            dma((7,)), dma((2,)),
            dma((2 * reach,)), dma((2 * reach,)),
            dma((2 * reach,)), dma((2 * reach,)),
            dma((2 * hops,)), dma((2 * hops,)),
            dma((4,)), dma((4,)),
            dma((n_x,)), dma((n_x,)),
            dma((14,)), dma((14,)),
        ],
        compiler_params=pltpu.CompilerParams(
            collective_id=0, has_side_effects=True, vmem_limit_bytes=56 * 1024 * 1024
        ),
    )(q, k, v, o, g, kp, vp, doc_lengths.reshape(1, -1))
    return pl.pallas_call(
        hand_over,
        out_shape=(
            jax.ShapeDtypeStruct(dq.shape, BF16),
            jax.ShapeDtypeStruct(gi.shape, BF16),
        ),
        in_specs=[pl.BlockSpec(memory_space=pltpu.VMEM)] * 2,
        out_specs=(any_spec, any_spec),
        scratch_shapes=[dma((2,))],
    )(dq, gi)


def build(mesh, n_x):
    return jax.shard_map(
        functools.partial(body, mesh.shape["ctx"], mesh.shape["head"], n_x),
        mesh=mesh,
        in_specs=(
            P("ctx", "head"),
            P("ctx", "head"),
            P("ctx", "head"),
            P("ctx", "head"),
            P("ctx", "head"),
            P(None, "head"),
            P(None, "head"),
            P(),
        ),
        out_specs=(P("ctx", "head"), P("head", "ctx")),
        check_vma=False,
    )


def solution(mesh):
    return build(mesh, X_CHIPS)
```

```python
import functools

import jax
import jax.numpy as jnp
from jax import lax
from jax.experimental import pallas as pl
from jax.experimental.pallas import tpu as pltpu
from jax.sharding import PartitionSpec as P

MESH = pl.DeviceIdType.MESH
HEAD_SIZE = 128
BLOCK_ROWS = 128
LONGEST_ROWS = 1024
X_CHIPS = 4
NEG_BIG = -1.0e30
LOG2E = 1.4426950408889634

F32 = jnp.float32
BF16 = jnp.bfloat16


def dot_nn(a, b):
    return lax.dot_general(a, b, (((1,), (0,)), ((), ())), preferred_element_type=F32)


def dot_nt(a, b):
    return lax.dot_general(a, b, (((1,), (1,)), ((), ())), preferred_element_type=F32)


def kernel(
    n_ctx, n_y, n_x,
    q_hbm, k_hbm, v_hbm, o_hbm, g_hbm, kp_hbm, vp_hbm, doc_ref,
    dq_hbm, gi_hbm,
    q_ref, g_ref, o_ref, qt_ref, gt_ref, kwin, vwin, bias_ref, p_ref, ds_ref,
    w_ref, all_ref, term_ref, inbox_ref, own_ref, acc_ref, dq_ref, gi_ref,
    load_sem, out_sem, ctx_send, ctx_recv, term_send, term_recv,
    wy_send, wy_recv, wx_send, wx_recv, wc_send, wc_recv, ay_send, ay_recv,
):
    rows, width = q_hbm.shape
    heads = width // HEAD_SIZE
    back = LONGEST_ROWS - BLOCK_ROWS
    win = back + rows
    reach = LONGEST_ROWS // rows
    model_rows = gi_hbm.shape[0]
    part_rows = model_rows // (2 * n_x)
    scale = HEAD_SIZE ** -0.5

    c = lax.axis_index("ctx")
    y = lax.axis_index("head")
    per_x = n_ctx // n_x
    x = c // per_x
    inner = c % per_x
    core = c % 2
    peer = c + 1 - 2 * core

    def at_ctx(i):
        return (lax.rem(c + i + n_ctx, n_ctx), y)

    def at_y(i):
        return (c, lax.rem(y + i + n_y, n_y))

    def at_x(i):
        return (lax.rem(x + i, n_x) * per_x + inner, y)

    def remote(src, dst, send, recv, to):
        return pltpu.make_async_remote_copy(
            src_ref=src, dst_ref=dst, send_sem=send, recv_sem=recv, device_id=to, device_id_type=MESH
        )

    loads = [
        pltpu.make_async_copy(k_hbm, kwin.at[pl.ds(back, rows), :], load_sem.at[0]),
        pltpu.make_async_copy(v_hbm, vwin.at[pl.ds(back, rows), :], load_sem.at[1]),
        pltpu.make_async_copy(q_hbm, q_ref, load_sem.at[2]),
        pltpu.make_async_copy(g_hbm, g_ref, load_sem.at[3]),
        pltpu.make_async_copy(o_hbm, o_ref, load_sem.at[4]),
    ]
    my_part = pl.multiple_of((x * 2 + core) * part_rows, part_rows)
    my_rows = pl.multiple_of(y * model_rows + my_part, part_rows)
    for kv, src in ((0, kp_hbm), (1, vp_hbm)):
        loads.append(pltpu.make_async_copy(
            src.at[pl.ds(my_rows, part_rows), :],
            w_ref.at[kv, y, pl.ds(my_part, part_rows), :],
            load_sem.at[5 + kv],
        ))
    for copy in loads:
        copy.start()

    loads[0].wait()
    loads[1].wait()
    barrier = pltpu.get_barrier_semaphore()
    partners = [at_ctx(i) for i in range(-reach, reach + 1) if i != 0]
    partners += [at_y(i) for i in range(1, n_y)] + [at_x(i) for i in range(1, n_x)]
    for to in partners:
        pl.semaphore_signal(barrier, inc=1, device_id=to, device_id_type=MESH)
    pl.semaphore_wait(barrier, len(partners))

    def context_copies(kv, ref):
        copies = []
        for i in range(1, reach + 1):
            first = max(back - i * rows, 0)
            cut = max(i * rows - back, 0)
            copies.append(remote(
                ref.at[pl.ds(back + cut, rows - cut), :], ref.at[pl.ds(first, rows - cut), :],
                ctx_send.at[kv * reach + i - 1], ctx_recv.at[kv * reach + i - 1], at_ctx(i),
            ))
        return copies

    key_copies = context_copies(0, kwin)
    value_copies = context_copies(1, vwin)
    for copy in key_copies:
        copy.start()

    wy_copies = []
    for i in (1, 7, 2, 6, 3, 5, 4):
        other = lax.rem(y + i, n_y)
        theirs = pl.multiple_of(other * model_rows + my_part, part_rows)
        for kv, src in ((0, kp_hbm), (1, vp_hbm)):
            wy_copies.append(remote(
                src.at[pl.ds(theirs, part_rows), :],
                w_ref.at[kv, y, pl.ds(my_part, part_rows), :],
                wy_send.at[2 * (i - 1) + kv], wy_recv.at[2 * (i - 1) + kv], at_y(i),
            ))
    for copy in wy_copies[:8]:
        copy.start()

    def row_part(i):
        first = (lax.rem(x + i + n_x, n_x) * 2 + core) * part_rows
        return pl.ds(pl.multiple_of(first, part_rows), part_rows)

    wx_copies = []

    def pass_on(group):
        mine = w_ref.at[:, lax.rem(y + group, n_y), row_part(0), :]
        for i in (1, n_x - 1):
            k = len(wx_copies)
            wx_copies.append(remote(mine, mine, wx_send.at[k], wx_recv.at[k], at_x(i)))
            wx_copies[-1].start()

    def take_in(distances):
        for i in distances:
            k = 2 * (1, 7, 2, 6, 3, 5, 4).index(i)
            wy_copies[k].wait_recv()
            wy_copies[k + 1].wait_recv()
            pass_on(n_y - i)

    loads[5].wait()
    loads[6].wait()
    pass_on(0)

    docs = doc_ref.shape[1]
    lens = jnp.broadcast_to(doc_ref[...].astype(F32), (docs, docs))
    sub = lax.broadcasted_iota(jnp.int32, (docs, docs), 0)
    lane = lax.broadcasted_iota(jnp.int32, (docs, docs), 1)
    lens_col = jnp.sum(jnp.where(sub == lane, lens, 0.0), axis=1, keepdims=True)
    starts = jnp.sum(jnp.where(sub < lane, lens_col, 0.0), axis=0, keepdims=True)
    row_abs = (lax.broadcasted_iota(jnp.int32, (rows, docs), 0) + c * rows).astype(F32)
    row_start = jnp.max(jnp.where(starts <= row_abs, starts, 0.0), axis=1, keepdims=True)
    row_id = lax.broadcasted_iota(jnp.int32, (rows, 1), 0)
    low = row_start - (row_id + c * rows).astype(F32) + row_id.astype(F32)
    low = jnp.maximum(low, ((row_id // BLOCK_ROWS) * BLOCK_ROWS - back).astype(F32))
    for first in range(0, win, 128):
        key_rel = (lax.broadcasted_iota(jnp.int32, (rows, 128), 1) + (first - back)).astype(F32)
        seen = (key_rel <= row_id.astype(F32)) & (key_rel >= low)
        bias_ref[:, first:first + 128] = jnp.where(seen, 0.0, NEG_BIG)

    def clear_head(h, _):
        for b in range(rows // BLOCK_ROWS):
            rows_at = pl.ds(pl.multiple_of(h * rows + b * BLOCK_ROWS, BLOCK_ROWS), BLOCK_ROWS)
            for first in range(0, win, BLOCK_ROWS):
                if first < b * BLOCK_ROWS or first >= b * BLOCK_ROWS + LONGEST_ROWS:
                    for ref in (p_ref, ds_ref):
                        ref[rows_at, first:first + BLOCK_ROWS] = jnp.zeros((BLOCK_ROWS, BLOCK_ROWS), BF16)
        return 0

    lax.fori_loop(0, heads, clear_head, 0)

    loads[2].wait()
    loads[3].wait()
    for h in range(heads):
        cols = slice(h * HEAD_SIZE, (h + 1) * HEAD_SIZE)
        qt_ref[:, h * rows:(h + 1) * rows] = q_ref[:, cols].T
        gt_ref[:, h * rows:(h + 1) * rows] = g_ref[:, cols].T

    take_in((1, 7, 2, 6))
    for copy in wy_copies[8:]:
        copy.start()
    for near, far in zip(key_copies, value_copies):
        near.wait_recv()
        far.start()

    def head_cols(h):
        return pl.ds(pl.multiple_of(h * HEAD_SIZE, HEAD_SIZE), HEAD_SIZE)

    def head_rows(h):
        return pl.ds(pl.multiple_of(h * rows, rows), rows)

    def block_of(h, b):
        rows_at = pl.ds(pl.multiple_of(h * rows + b * BLOCK_ROWS, BLOCK_ROWS), BLOCK_ROWS)
        here = slice(b * BLOCK_ROWS, (b + 1) * BLOCK_ROWS)
        return rows_at, here, slice(b * BLOCK_ROWS, b * BLOCK_ROWS + LONGEST_ROWS)

    def softmax_head(h, _):
        for b in range(rows // BLOCK_ROWS):
            rows_at, here, keys = block_of(h, b)
            s = dot_nt(q_ref[here, head_cols(h)], kwin[keys, :]) * (scale * LOG2E) + bias_ref[here, keys]
            top = jnp.max(s, axis=1, keepdims=True)
            e = jnp.exp2(s - top)
            total = jnp.sum(e, axis=1, keepdims=True)
            p_ref[rows_at, keys] = (e * (1.0 / total)).astype(BF16)
        return 0

    lax.fori_loop(0, heads, softmax_head, 0, unroll=4)

    chunks = [(0, rows - (reach * rows - back), reach)]
    chunks += [(back - i * rows, rows, i) for i in range(reach - 1, -1, -1)]

    def term_copies(kv):
        copies = []
        for first, size, i in chunks[:-1]:
            copies.append(remote(
                term_ref.at[kv, i - 1, :, pl.ds(rows - size, size)],
                inbox_ref.at[kv, i - 1, :, pl.ds(rows - size, size)],
                term_send.at[kv * reach + i - 1], term_recv.at[kv * reach + i - 1], at_ctx(-i),
            ))
        return copies

    def terms(kv, left_ref, right_ref, factor):
        copies = term_copies(kv)
        for (first, size, i), copy in zip(chunks, copies + [None]):
            part = dot_nn(left_ref[...], right_ref[:, first:first + size])
            if factor != 1.0:
                part = part * factor
            if i > 0:
                term_ref[kv, i - 1, :, rows - size:] = part.astype(BF16)
                copy.start()
            else:
                own_ref[kv] = part
        return copies

    value_terms = terms(1, gt_ref, p_ref, 1.0)

    before = w_ref.at[0, :, row_part(-1), :]
    after = w_ref.at[1, :, row_part(1), :]
    wx_far = [
        remote(before, before, wx_send.at[2 * n_y], wx_recv.at[2 * n_y], at_x(1)),
        remote(after, after, wx_send.at[2 * n_y + 1], wx_recv.at[2 * n_y + 1], at_x(n_x - 1)),
    ]
    wc_copies = []
    for k, i in enumerate((0, -1, 1, 2)):
        part = w_ref.at[:, :, row_part(i), :]
        wc_copies.append(remote(part, part, wc_send.at[k], wc_recv.at[k], (peer, y)))
    loads[4].wait()
    for copy in value_copies:
        copy.wait_recv()

    def score_head(h, _):
        grad = g_ref[:, head_cols(h)]
        delta = jnp.sum(grad.astype(F32) * o_ref[:, head_cols(h)].astype(F32), axis=1, keepdims=True)
        for b in range(rows // BLOCK_ROWS):
            rows_at, here, keys = block_of(h, b)
            dp = dot_nt(grad[here, :], vwin[keys, :])
            ds_ref[rows_at, keys] = (p_ref[rows_at, keys].astype(F32) * (dp - delta[here, :])).astype(BF16)
        return 0

    def query_head(h, _):
        for b in range(rows // BLOCK_ROWS):
            rows_at, here, keys = block_of(h, b)
            dq = dot_nn(ds_ref[rows_at, keys], kwin[keys, :]) * scale
            dq_ref[here, head_cols(h)] = dq.astype(BF16)
        return 0

    def own_sum(kv, copies):
        for copy in copies:
            copy.wait_recv()
        total = own_ref[kv]
        for i in range(1, reach):
            total = total + inbox_ref[kv, i - 1].astype(F32)
        size = chunks[0][1]
        cut = rows - size
        last = total[:, cut:] + inbox_ref[kv, reach - 1, :, cut:].astype(F32)
        slab = kv * n_y + y
        all_ref[slab, :, :cut] = total[:, :cut].astype(BF16)
        all_ref[slab, :, cut:] = last.astype(BF16)


    way = 1 - 2 * core

    def slab_at(kv, i):
        return kv * n_y + lax.rem(y + way * i + n_y, n_y)

    def gather_copies(kv):
        copies = []
        for k, (i, j) in enumerate(((0, 2), (0, -2), (0, 1), (0, -1), (-2, 1), (2, -1), (-2, 2))):
            slab = all_ref.at[slab_at(kv, i)]
            copies.append(remote(slab, slab, ay_send.at[kv * 7 + k], ay_recv.at[kv * 7 + k], at_y(way * j)))
        return copies

    def gather_first(copies):
        for copy in copies[:4]:
            copy.start()

    def gather_second(copies):
        copies[0].wait_recv()
        copies[4].start()
        copies[1].wait_recv()
        copies[5].start()
        copies[6].start()

    lax.fori_loop(0, heads, score_head, 0, unroll=4)
    key_terms = terms(0, qt_ref, ds_ref, scale)
    take_in((3, 5, 4))
    wc_copies[0].start()
    own_sum(1, value_terms)
    value_gather = gather_copies(1)
    gather_first(value_gather)
    lax.fori_loop(0, heads // 2, query_head, 0, unroll=4)
    gather_second(value_gather)
    lax.fori_loop(heads // 2, heads, query_head, 0, unroll=4)
    dq_out = pltpu.make_async_copy(dq_ref, dq_hbm, out_sem.at[0])
    dq_out.start()
    for copy in wx_copies:
        copy.wait_recv()
    for copy in wx_far + wc_copies[1:3]:
        copy.start()
    own_sum(0, key_terms)
    key_gather = gather_copies(0)
    gather_first(key_gather)
    tile = 256
    tiles = model_rows // tile

    def project(kv, t, slabs):
        row = pl.ds(pl.multiple_of(t * tile, tile), tile)
        left = jnp.concatenate([w_ref[kv, g, row, :] for g in slabs], axis=1)
        right = jnp.concatenate([all_ref[kv * n_y + g] for g in slabs], axis=0)
        return row, dot_nn(left, right)

    def project_values(t, _):
        row, part = project(1, t, range(n_y))
        acc_ref[row, :] = part
        return 0

    def project_near(t, _):
        row, part = project(0, t, [slab_at(0, i) for i in (-2, 2, 0, -1, 1)])
        acc_ref[row, :] = acc_ref[row, :] + part
        return 0

    def project_far(t, _):
        row, part = project(0, t, [slab_at(0, i) for i in (-3, 3, 4)])
        gi_ref[row, :] = (acc_ref[row, :] + part).astype(BF16)
        return 0

    gather_second(key_gather)
    for copy in wx_far:
        copy.wait_recv()
    wc_copies[3].start()
    for copy in value_gather[2:] + wc_copies:
        copy.wait_recv()
    lax.fori_loop(0, tiles, project_values, 0)
    key_gather[2].wait_recv()
    key_gather[3].wait_recv()
    lax.fori_loop(0, tiles, project_near, 0)
    for copy in key_gather[4:]:
        copy.wait_recv()
    lax.fori_loop(0, tiles, project_far, 0)
    gi_out = pltpu.make_async_copy(gi_ref, gi_hbm, out_sem.at[1])
    gi_out.start()

    for copy in key_copies + value_copies + wy_copies + wx_copies + wx_far + wc_copies + value_terms + key_terms + value_gather + key_gather:
        copy.wait_send()
    dq_out.wait()
    gi_out.wait()


def hand_over(dq_in, gi_in, dq_out, gi_out, sem):
    copies = [
        pltpu.make_async_copy(dq_in, dq_out, sem.at[0]),
        pltpu.make_async_copy(gi_in, gi_out, sem.at[1]),
    ]
    for copy in copies:
        copy.start()
    for copy in copies:
        copy.wait()


def body(n_ctx, n_y, n_x, q, k, v, o, g, kp, vp, doc_lengths):
    rows, width = q.shape
    heads = width // HEAD_SIZE
    model_rows = kp.shape[0] // n_y
    reach = LONGEST_ROWS // rows
    win = LONGEST_ROWS - BLOCK_ROWS + rows
    hops = n_y - 1
    dma = pltpu.SemaphoreType.DMA
    any_spec = pl.BlockSpec(memory_space=pl.ANY)
    dq, gi = pl.pallas_call(
        functools.partial(kernel, n_ctx, n_y, n_x),
        out_shape=(
            jax.ShapeDtypeStruct((rows, width), BF16),
            jax.ShapeDtypeStruct((model_rows, rows), BF16),
        ),
        in_specs=[any_spec] * 7 + [pl.BlockSpec(memory_space=pltpu.VMEM)],
        out_specs=(any_spec, any_spec),
        scratch_shapes=[
            pltpu.VMEM((rows, width), BF16),
            pltpu.VMEM((rows, width), BF16),
            pltpu.VMEM((rows, width), BF16),
            pltpu.VMEM((HEAD_SIZE, heads * rows), BF16),
            pltpu.VMEM((HEAD_SIZE, heads * rows), BF16),
            pltpu.VMEM((win, HEAD_SIZE), BF16),
            pltpu.VMEM((win, HEAD_SIZE), BF16),
            pltpu.VMEM((rows, win), F32),
            pltpu.VMEM((heads * rows, win), BF16),
            pltpu.VMEM((heads * rows, win), BF16),
            pltpu.VMEM((2, n_y, model_rows, HEAD_SIZE), BF16),
            pltpu.VMEM((2 * n_y, HEAD_SIZE, rows), BF16),
            pltpu.VMEM((2, reach, HEAD_SIZE, rows), BF16),
            pltpu.VMEM((2, reach, HEAD_SIZE, rows), BF16),
            pltpu.VMEM((2, HEAD_SIZE, rows), F32),
            pltpu.VMEM((model_rows, rows), F32),
            pltpu.VMEM((rows, width), BF16),
            pltpu.VMEM((model_rows, rows), BF16),
            dma((7,)), dma((2,)),
            dma((2 * reach,)), dma((2 * reach,)),
            dma((2 * reach,)), dma((2 * reach,)),
            dma((2 * hops,)), dma((2 * hops,)),
            dma((2 * n_y + 2,)), dma((2 * n_y + 2,)),
            dma((n_x,)), dma((n_x,)),
            dma((14,)), dma((14,)),
        ],
        compiler_params=pltpu.CompilerParams(
            collective_id=0, has_side_effects=True, vmem_limit_bytes=56 * 1024 * 1024
        ),
    )(q, k, v, o, g, kp, vp, doc_lengths.reshape(1, -1))
    return pl.pallas_call(
        hand_over,
        out_shape=(
            jax.ShapeDtypeStruct(dq.shape, BF16),
            jax.ShapeDtypeStruct(gi.shape, BF16),
        ),
        in_specs=[pl.BlockSpec(memory_space=pltpu.VMEM)] * 2,
        out_specs=(any_spec, any_spec),
        scratch_shapes=[dma((2,))],
    )(dq, gi)


def build(mesh, n_x):
    return jax.shard_map(
        functools.partial(body, mesh.shape["ctx"], mesh.shape["head"], n_x),
        mesh=mesh,
        in_specs=(
            P("ctx", "head"),
            P("ctx", "head"),
            P("ctx", "head"),
            P("ctx", "head"),
            P("ctx", "head"),
            P(None, "head"),
            P(None, "head"),
            P(),
        ),
        out_specs=(P("ctx", "head"), P("head", "ctx")),
        check_vma=False,
    )


def solution(mesh):
    return build(mesh, X_CHIPS)
```

```python
import functools

import jax
import jax.numpy as jnp
from jax import lax
from jax.experimental import pallas as pl
from jax.experimental.pallas import tpu as pltpu
from jax.sharding import PartitionSpec as P

MESH = pl.DeviceIdType.MESH
HEAD_SIZE = 128
BLOCK_ROWS = 128
LONGEST_ROWS = 1024
X_CHIPS = 4
NEG_BIG = -1.0e30
LOG2E = 1.4426950408889634

F32 = jnp.float32
BF16 = jnp.bfloat16


def dot_nn(a, b):
    return lax.dot_general(a, b, (((1,), (0,)), ((), ())), preferred_element_type=F32)


def dot_nt(a, b):
    return lax.dot_general(a, b, (((1,), (1,)), ((), ())), preferred_element_type=F32)


def kernel(
    n_ctx, n_y, n_x,
    q_hbm, k_hbm, v_hbm, o_hbm, g_hbm, kp_hbm, vp_hbm, doc_ref,
    dq_hbm, gi_hbm,
    q_ref, g_ref, o_ref, qt_ref, gt_ref, kwin, vwin, bias_ref, p_ref, ds_ref,
    w_ref, all_ref, term_ref, inbox_ref, own_ref, acc_ref, dq_ref, gi_ref,
    load_sem, out_sem, ctx_send, ctx_recv, term_send, term_recv,
    wy_send, wy_recv, wx_send, wx_recv, wc_send, wc_recv, ay_send, ay_recv,
):
    rows, width = q_hbm.shape
    heads = width // HEAD_SIZE
    back = LONGEST_ROWS - BLOCK_ROWS
    win = back + rows
    reach = LONGEST_ROWS // rows
    model_rows = gi_hbm.shape[0]
    part_rows = model_rows // (2 * n_x)
    scale = HEAD_SIZE ** -0.5

    c = lax.axis_index("ctx")
    y = lax.axis_index("head")
    per_x = n_ctx // n_x
    x = c // per_x
    inner = c % per_x
    core = c % 2
    peer = c + 1 - 2 * core

    def at_ctx(i):
        return (lax.rem(c + i + n_ctx, n_ctx), y)

    def at_y(i):
        return (c, lax.rem(y + i + n_y, n_y))

    def at_x(i):
        return (lax.rem(x + i, n_x) * per_x + inner, y)

    def remote(src, dst, send, recv, to):
        return pltpu.make_async_remote_copy(
            src_ref=src, dst_ref=dst, send_sem=send, recv_sem=recv, device_id=to, device_id_type=MESH
        )

    loads = [
        pltpu.make_async_copy(k_hbm, kwin.at[pl.ds(back, rows), :], load_sem.at[0]),
        pltpu.make_async_copy(v_hbm, vwin.at[pl.ds(back, rows), :], load_sem.at[1]),
        pltpu.make_async_copy(q_hbm, q_ref, load_sem.at[2]),
        pltpu.make_async_copy(g_hbm, g_ref, load_sem.at[3]),
        pltpu.make_async_copy(o_hbm, o_ref, load_sem.at[4]),
    ]
    my_part = pl.multiple_of((x * 2 + core) * part_rows, part_rows)
    my_rows = pl.multiple_of(y * model_rows + my_part, part_rows)
    for kv, src in ((0, kp_hbm), (1, vp_hbm)):
        loads.append(pltpu.make_async_copy(
            src.at[pl.ds(my_rows, part_rows), :],
            w_ref.at[kv, y, pl.ds(my_part, part_rows), :],
            load_sem.at[5 + kv],
        ))
    for copy in loads:
        copy.start()

    loads[0].wait()
    loads[1].wait()
    barrier = pltpu.get_barrier_semaphore()
    partners = [at_ctx(i) for i in range(-reach, reach + 1) if i != 0]
    partners += [at_y(i) for i in range(1, n_y)] + [at_x(i) for i in range(1, n_x)]
    for to in partners:
        pl.semaphore_signal(barrier, inc=1, device_id=to, device_id_type=MESH)
    pl.semaphore_wait(barrier, len(partners))

    def context_copies(kv, ref):
        copies = []
        for i in range(1, reach + 1):
            first = max(back - i * rows, 0)
            cut = max(i * rows - back, 0)
            copies.append(remote(
                ref.at[pl.ds(back + cut, rows - cut), :], ref.at[pl.ds(first, rows - cut), :],
                ctx_send.at[kv * reach + i - 1], ctx_recv.at[kv * reach + i - 1], at_ctx(i),
            ))
        return copies

    key_copies = context_copies(0, kwin)
    value_copies = context_copies(1, vwin)
    for copy in key_copies:
        copy.start()

    wy_copies = []
    for i in (1, 7, 2, 6, 3, 5, 4):
        other = lax.rem(y + i, n_y)
        theirs = pl.multiple_of(other * model_rows + my_part, part_rows)
        for kv, src in ((0, kp_hbm), (1, vp_hbm)):
            wy_copies.append(remote(
                src.at[pl.ds(theirs, part_rows), :],
                w_ref.at[kv, y, pl.ds(my_part, part_rows), :],
                wy_send.at[2 * (i - 1) + kv], wy_recv.at[2 * (i - 1) + kv], at_y(i),
            ))
    for copy in wy_copies[:8]:
        copy.start()

    def row_part(i):
        first = (lax.rem(x + i + n_x, n_x) * 2 + core) * part_rows
        return pl.ds(pl.multiple_of(first, part_rows), part_rows)

    wx_copies = []

    def pass_on(group):
        mine = w_ref.at[:, lax.rem(y + group, n_y), row_part(0), :]
        for i in (1, n_x - 1):
            k = len(wx_copies)
            wx_copies.append(remote(mine, mine, wx_send.at[k], wx_recv.at[k], at_x(i)))
            wx_copies[-1].start()

    def take_in(distances):
        for i in distances:
            k = 2 * (1, 7, 2, 6, 3, 5, 4).index(i)
            wy_copies[k].wait_recv()
            wy_copies[k + 1].wait_recv()
            pass_on(n_y - i)

    wx_far = []

    def relay(turns):
        for t in turns:
            slab = lax.rem(y + (0, 7, 1, 6, 2, 5, 3, 4)[t], n_y)
            for kv, i, to in ((0, -1, 1), (1, 1, n_x - 1)):
                wx_copies[2 * t + kv].wait_recv()
                part = w_ref.at[kv, slab, row_part(i), :]
                k = 2 * n_y + 2 * t + kv
                wx_far.append(remote(part, part, wx_send.at[k], wx_recv.at[k], at_x(to)))
                wx_far[-1].start()

    loads[5].wait()
    loads[6].wait()
    pass_on(0)

    docs = doc_ref.shape[1]
    lens = jnp.broadcast_to(doc_ref[...].astype(F32), (docs, docs))
    sub = lax.broadcasted_iota(jnp.int32, (docs, docs), 0)
    lane = lax.broadcasted_iota(jnp.int32, (docs, docs), 1)
    lens_col = jnp.sum(jnp.where(sub == lane, lens, 0.0), axis=1, keepdims=True)
    starts = jnp.sum(jnp.where(sub < lane, lens_col, 0.0), axis=0, keepdims=True)
    row_abs = (lax.broadcasted_iota(jnp.int32, (rows, docs), 0) + c * rows).astype(F32)
    row_start = jnp.max(jnp.where(starts <= row_abs, starts, 0.0), axis=1, keepdims=True)
    row_id = lax.broadcasted_iota(jnp.int32, (rows, 1), 0)
    low = row_start - (row_id + c * rows).astype(F32) + row_id.astype(F32)
    low = jnp.maximum(low, ((row_id // BLOCK_ROWS) * BLOCK_ROWS - back).astype(F32))
    for first in range(0, win, 128):
        key_rel = (lax.broadcasted_iota(jnp.int32, (rows, 128), 1) + (first - back)).astype(F32)
        seen = (key_rel <= row_id.astype(F32)) & (key_rel >= low)
        bias_ref[:, first:first + 128] = jnp.where(seen, 0.0, NEG_BIG)

    def clear_head(h, _):
        for b in range(rows // BLOCK_ROWS):
            rows_at = pl.ds(pl.multiple_of(h * rows + b * BLOCK_ROWS, BLOCK_ROWS), BLOCK_ROWS)
            for first in range(0, win, BLOCK_ROWS):
                if first < b * BLOCK_ROWS or first >= b * BLOCK_ROWS + LONGEST_ROWS:
                    for ref in (p_ref, ds_ref):
                        ref[rows_at, first:first + BLOCK_ROWS] = jnp.zeros((BLOCK_ROWS, BLOCK_ROWS), BF16)
        return 0

    lax.fori_loop(0, heads, clear_head, 0)

    loads[2].wait()
    loads[3].wait()
    for h in range(heads):
        cols = slice(h * HEAD_SIZE, (h + 1) * HEAD_SIZE)
        qt_ref[:, h * rows:(h + 1) * rows] = q_ref[:, cols].T
        gt_ref[:, h * rows:(h + 1) * rows] = g_ref[:, cols].T

    take_in((1, 7, 2, 6))
    for copy in wy_copies[8:]:
        copy.start()
    for near, far in zip(key_copies, value_copies):
        near.wait_recv()
        far.start()

    def head_cols(h):
        return pl.ds(pl.multiple_of(h * HEAD_SIZE, HEAD_SIZE), HEAD_SIZE)

    def head_rows(h):
        return pl.ds(pl.multiple_of(h * rows, rows), rows)

    def block_of(h, b):
        rows_at = pl.ds(pl.multiple_of(h * rows + b * BLOCK_ROWS, BLOCK_ROWS), BLOCK_ROWS)
        here = slice(b * BLOCK_ROWS, (b + 1) * BLOCK_ROWS)
        return rows_at, here, slice(b * BLOCK_ROWS, b * BLOCK_ROWS + LONGEST_ROWS)

    def softmax_head(h, _):
        for b in range(rows // BLOCK_ROWS):
            rows_at, here, keys = block_of(h, b)
            s = dot_nt(q_ref[here, head_cols(h)], kwin[keys, :]) * (scale * LOG2E) + bias_ref[here, keys]
            top = jnp.max(s, axis=1, keepdims=True)
            e = jnp.exp2(s - top)
            total = jnp.sum(e, axis=1, keepdims=True)
            p_ref[rows_at, keys] = (e * (1.0 / total)).astype(BF16)
        return 0

    lax.fori_loop(0, heads, softmax_head, 0, unroll=4)

    chunks = [(0, rows - (reach * rows - back), reach)]
    chunks += [(back - i * rows, rows, i) for i in range(reach - 1, -1, -1)]

    def term_copies(kv):
        copies = []
        for first, size, i in chunks[:-1]:
            copies.append(remote(
                term_ref.at[kv, i - 1, :, pl.ds(rows - size, size)],
                inbox_ref.at[kv, i - 1, :, pl.ds(rows - size, size)],
                term_send.at[kv * reach + i - 1], term_recv.at[kv * reach + i - 1], at_ctx(-i),
            ))
        return copies

    def terms(kv, left_ref, right_ref, factor):
        copies = term_copies(kv)
        for (first, size, i), copy in zip(chunks, copies + [None]):
            part = dot_nn(left_ref[...], right_ref[:, first:first + size])
            if factor != 1.0:
                part = part * factor
            if i > 0:
                term_ref[kv, i - 1, :, rows - size:] = part.astype(BF16)
                copy.start()
            else:
                own_ref[kv] = part
        return copies

    value_terms = terms(1, gt_ref, p_ref, 1.0)

    wc_copies = []
    for k, i in enumerate((0, -1, 1, 2)):
        part = w_ref.at[:, :, row_part(i), :]
        wc_copies.append(remote(part, part, wc_send.at[k], wc_recv.at[k], (peer, y)))
    loads[4].wait()
    for copy in value_copies:
        copy.wait_recv()
    relay(range(5))

    def score_head(h, _):
        grad = g_ref[:, head_cols(h)]
        delta = jnp.sum(grad.astype(F32) * o_ref[:, head_cols(h)].astype(F32), axis=1, keepdims=True)
        for b in range(rows // BLOCK_ROWS):
            rows_at, here, keys = block_of(h, b)
            dp = dot_nt(grad[here, :], vwin[keys, :])
            ds_ref[rows_at, keys] = (p_ref[rows_at, keys].astype(F32) * (dp - delta[here, :])).astype(BF16)
        return 0

    def query_head(h, _):
        for b in range(rows // BLOCK_ROWS):
            rows_at, here, keys = block_of(h, b)
            dq = dot_nn(ds_ref[rows_at, keys], kwin[keys, :]) * scale
            dq_ref[here, head_cols(h)] = dq.astype(BF16)
        return 0

    def own_sum(kv, copies):
        for copy in copies:
            copy.wait_recv()
        total = own_ref[kv]
        for i in range(1, reach):
            total = total + inbox_ref[kv, i - 1].astype(F32)
        size = chunks[0][1]
        cut = rows - size
        last = total[:, cut:] + inbox_ref[kv, reach - 1, :, cut:].astype(F32)
        slab = kv * n_y + y
        all_ref[slab, :, :cut] = total[:, :cut].astype(BF16)
        all_ref[slab, :, cut:] = last.astype(BF16)


    way = 1 - 2 * core

    def slab_at(kv, i):
        return kv * n_y + lax.rem(y + way * i + n_y, n_y)

    def gather_copies(kv):
        copies = []
        for k, (i, j) in enumerate(((0, 2), (0, -2), (0, 1), (0, -1), (-2, 1), (2, -1), (-2, 2))):
            slab = all_ref.at[slab_at(kv, i)]
            copies.append(remote(slab, slab, ay_send.at[kv * 7 + k], ay_recv.at[kv * 7 + k], at_y(way * j)))
        return copies

    def gather_first(copies):
        for copy in copies[:4]:
            copy.start()

    def gather_second(copies):
        copies[0].wait_recv()
        copies[4].start()
        copies[1].wait_recv()
        copies[5].start()
        copies[6].start()

    lax.fori_loop(0, heads // 2, score_head, 0, unroll=4)
    take_in((3, 5, 4))
    wc_copies[0].start()
    lax.fori_loop(heads // 2, heads, score_head, 0, unroll=4)
    key_terms = terms(0, qt_ref, ds_ref, scale)
    own_sum(1, value_terms)
    value_gather = gather_copies(1)
    gather_first(value_gather)
    lax.fori_loop(0, heads // 2, query_head, 0, unroll=4)
    gather_second(value_gather)
    relay(range(5, n_y))
    for copy in wc_copies[1:3]:
        copy.start()
    lax.fori_loop(heads // 2, heads, query_head, 0, unroll=4)
    dq_out = pltpu.make_async_copy(dq_ref, dq_hbm, out_sem.at[0])
    dq_out.start()
    own_sum(0, key_terms)
    key_gather = gather_copies(0)
    gather_first(key_gather)
    tile = 256
    tiles = model_rows // tile

    def project(kv, t, slabs):
        row = pl.ds(pl.multiple_of(t * tile, tile), tile)
        left = jnp.concatenate([w_ref[kv, g, row, :] for g in slabs], axis=1)
        right = jnp.concatenate([all_ref[kv * n_y + g] for g in slabs], axis=0)
        return row, dot_nn(left, right)

    def project_values(t, _):
        row, part = project(1, t, range(n_y))
        acc_ref[row, :] = part
        return 0

    def project_near(t, _):
        row, part = project(0, t, [slab_at(0, i) for i in (-2, 2, 0, -1, 1)])
        acc_ref[row, :] = acc_ref[row, :] + part
        return 0

    def project_far(t, _):
        row, part = project(0, t, [slab_at(0, i) for i in (-3, 3, 4)])
        gi_ref[row, :] = (acc_ref[row, :] + part).astype(BF16)
        return 0

    gather_second(key_gather)
    for copy in wx_far:
        copy.wait_recv()
    wc_copies[3].start()
    for copy in value_gather[2:] + wc_copies:
        copy.wait_recv()
    lax.fori_loop(0, tiles, project_values, 0)
    key_gather[2].wait_recv()
    key_gather[3].wait_recv()
    lax.fori_loop(0, tiles, project_near, 0)
    for copy in key_gather[4:]:
        copy.wait_recv()
    lax.fori_loop(0, tiles, project_far, 0)
    gi_out = pltpu.make_async_copy(gi_ref, gi_hbm, out_sem.at[1])
    gi_out.start()

    for copy in key_copies + value_copies + wy_copies + wx_copies + wx_far + wc_copies + value_terms + key_terms + value_gather + key_gather:
        copy.wait_send()
    dq_out.wait()
    gi_out.wait()


def hand_over(dq_in, gi_in, dq_out, gi_out, sem):
    copies = [
        pltpu.make_async_copy(dq_in, dq_out, sem.at[0]),
        pltpu.make_async_copy(gi_in, gi_out, sem.at[1]),
    ]
    for copy in copies:
        copy.start()
    for copy in copies:
        copy.wait()


def body(n_ctx, n_y, n_x, q, k, v, o, g, kp, vp, doc_lengths):
    rows, width = q.shape
    heads = width // HEAD_SIZE
    model_rows = kp.shape[0] // n_y
    reach = LONGEST_ROWS // rows
    win = LONGEST_ROWS - BLOCK_ROWS + rows
    hops = n_y - 1
    dma = pltpu.SemaphoreType.DMA
    any_spec = pl.BlockSpec(memory_space=pl.ANY)
    dq, gi = pl.pallas_call(
        functools.partial(kernel, n_ctx, n_y, n_x),
        out_shape=(
            jax.ShapeDtypeStruct((rows, width), BF16),
            jax.ShapeDtypeStruct((model_rows, rows), BF16),
        ),
        in_specs=[any_spec] * 7 + [pl.BlockSpec(memory_space=pltpu.VMEM)],
        out_specs=(any_spec, any_spec),
        scratch_shapes=[
            pltpu.VMEM((rows, width), BF16),
            pltpu.VMEM((rows, width), BF16),
            pltpu.VMEM((rows, width), BF16),
            pltpu.VMEM((HEAD_SIZE, heads * rows), BF16),
            pltpu.VMEM((HEAD_SIZE, heads * rows), BF16),
            pltpu.VMEM((win, HEAD_SIZE), BF16),
            pltpu.VMEM((win, HEAD_SIZE), BF16),
            pltpu.VMEM((rows, win), F32),
            pltpu.VMEM((heads * rows, win), BF16),
            pltpu.VMEM((heads * rows, win), BF16),
            pltpu.VMEM((2, n_y, model_rows, HEAD_SIZE), BF16),
            pltpu.VMEM((2 * n_y, HEAD_SIZE, rows), BF16),
            pltpu.VMEM((2, reach, HEAD_SIZE, rows), BF16),
            pltpu.VMEM((2, reach, HEAD_SIZE, rows), BF16),
            pltpu.VMEM((2, HEAD_SIZE, rows), F32),
            pltpu.VMEM((model_rows, rows), F32),
            pltpu.VMEM((rows, width), BF16),
            pltpu.VMEM((model_rows, rows), BF16),
            dma((7,)), dma((2,)),
            dma((2 * reach,)), dma((2 * reach,)),
            dma((2 * reach,)), dma((2 * reach,)),
            dma((2 * hops,)), dma((2 * hops,)),
            dma((4 * n_y,)), dma((4 * n_y,)),
            dma((n_x,)), dma((n_x,)),
            dma((14,)), dma((14,)),
        ],
        compiler_params=pltpu.CompilerParams(
            collective_id=0, has_side_effects=True, vmem_limit_bytes=56 * 1024 * 1024
        ),
    )(q, k, v, o, g, kp, vp, doc_lengths.reshape(1, -1))
    return pl.pallas_call(
        hand_over,
        out_shape=(
            jax.ShapeDtypeStruct(dq.shape, BF16),
            jax.ShapeDtypeStruct(gi.shape, BF16),
        ),
        in_specs=[pl.BlockSpec(memory_space=pltpu.VMEM)] * 2,
        out_specs=(any_spec, any_spec),
        scratch_shapes=[dma((2,))],
    )(dq, gi)


def build(mesh, n_x):
    return jax.shard_map(
        functools.partial(body, mesh.shape["ctx"], mesh.shape["head"], n_x),
        mesh=mesh,
        in_specs=(
            P("ctx", "head"),
            P("ctx", "head"),
            P("ctx", "head"),
            P("ctx", "head"),
            P("ctx", "head"),
            P(None, "head"),
            P(None, "head"),
            P(),
        ),
        out_specs=(P("ctx", "head"), P("head", "ctx")),
        check_vma=False,
    )


def solution(mesh):
    return build(mesh, X_CHIPS)
```

```python
import functools

import jax
import jax.numpy as jnp
from jax import lax
from jax.experimental import pallas as pl
from jax.experimental.pallas import tpu as pltpu
from jax.sharding import PartitionSpec as P

MESH = pl.DeviceIdType.MESH
HEAD_SIZE = 128
BLOCK_ROWS = 128
LONGEST_ROWS = 1024
X_CHIPS = 4
NEG_BIG = -1.0e30
LOG2E = 1.4426950408889634

F32 = jnp.float32
BF16 = jnp.bfloat16


def dot_nn(a, b):
    return lax.dot_general(a, b, (((1,), (0,)), ((), ())), preferred_element_type=F32)


def dot_nt(a, b):
    return lax.dot_general(a, b, (((1,), (1,)), ((), ())), preferred_element_type=F32)


def kernel(
    n_ctx, n_y, n_x,
    q_hbm, k_hbm, v_hbm, o_hbm, g_hbm, kp_hbm, vp_hbm, doc_ref,
    dq_hbm, gi_hbm,
    q_ref, g_ref, o_ref, qt_ref, gt_ref, kwin, vwin, bias_ref, p_ref, ds_ref,
    w_ref, all_ref, term_ref, inbox_ref, own_ref, acc_ref, dq_ref, gi_ref,
    load_sem, out_sem, ctx_send, ctx_recv, term_send, term_recv,
    wy_send, wy_recv, wx_send, wx_recv, wc_send, wc_recv, ay_send, ay_recv,
):
    rows, width = q_hbm.shape
    heads = width // HEAD_SIZE
    back = LONGEST_ROWS - BLOCK_ROWS
    win = back + rows
    reach = LONGEST_ROWS // rows
    model_rows = gi_hbm.shape[0]
    part_rows = model_rows // (2 * n_x)
    scale = HEAD_SIZE ** -0.5

    c = lax.axis_index("ctx")
    y = lax.axis_index("head")
    per_x = n_ctx // n_x
    x = c // per_x
    inner = c % per_x
    core = c % 2
    peer = c + 1 - 2 * core

    def at_ctx(i):
        return (lax.rem(c + i + n_ctx, n_ctx), y)

    def at_y(i):
        return (c, lax.rem(y + i + n_y, n_y))

    def at_x(i):
        return (lax.rem(x + i, n_x) * per_x + inner, y)

    def remote(src, dst, send, recv, to):
        return pltpu.make_async_remote_copy(
            src_ref=src, dst_ref=dst, send_sem=send, recv_sem=recv, device_id=to, device_id_type=MESH
        )

    loads = [
        pltpu.make_async_copy(k_hbm, kwin.at[pl.ds(back, rows), :], load_sem.at[0]),
        pltpu.make_async_copy(v_hbm, vwin.at[pl.ds(back, rows), :], load_sem.at[1]),
        pltpu.make_async_copy(q_hbm, q_ref, load_sem.at[2]),
        pltpu.make_async_copy(g_hbm, g_ref, load_sem.at[3]),
        pltpu.make_async_copy(o_hbm, o_ref, load_sem.at[4]),
    ]
    my_part = pl.multiple_of((x * 2 + core) * part_rows, part_rows)
    my_rows = pl.multiple_of(y * model_rows + my_part, part_rows)
    for kv, src in ((0, kp_hbm), (1, vp_hbm)):
        loads.append(pltpu.make_async_copy(
            src.at[pl.ds(my_rows, part_rows), :],
            w_ref.at[kv, y, pl.ds(my_part, part_rows), :],
            load_sem.at[5 + kv],
        ))
    for copy in loads:
        copy.start()

    loads[0].wait()
    loads[1].wait()
    barrier = pltpu.get_barrier_semaphore()
    partners = [at_ctx(i) for i in range(-reach, reach + 1) if i != 0]
    partners += [at_y(i) for i in range(1, n_y)] + [at_x(i) for i in range(1, n_x)]
    for to in partners:
        pl.semaphore_signal(barrier, inc=1, device_id=to, device_id_type=MESH)
    pl.semaphore_wait(barrier, len(partners))

    def context_copies(kv, ref):
        copies = []
        for i in range(1, reach + 1):
            first = max(back - i * rows, 0)
            cut = max(i * rows - back, 0)
            copies.append(remote(
                ref.at[pl.ds(back + cut, rows - cut), :], ref.at[pl.ds(first, rows - cut), :],
                ctx_send.at[kv * reach + i - 1], ctx_recv.at[kv * reach + i - 1], at_ctx(i),
            ))
        return copies

    key_copies = context_copies(0, kwin)
    value_copies = context_copies(1, vwin)
    for copy in key_copies:
        copy.start()

    wy_copies = []
    for i in (1, 7, 2, 6, 3, 5, 4):
        other = lax.rem(y + i, n_y)
        theirs = pl.multiple_of(other * model_rows + my_part, part_rows)
        for kv, src in ((0, kp_hbm), (1, vp_hbm)):
            wy_copies.append(remote(
                src.at[pl.ds(theirs, part_rows), :],
                w_ref.at[kv, y, pl.ds(my_part, part_rows), :],
                wy_send.at[2 * (i - 1) + kv], wy_recv.at[2 * (i - 1) + kv], at_y(i),
            ))
    for copy in wy_copies[:8]:
        copy.start()

    def row_part(i):
        first = (lax.rem(x + i + n_x, n_x) * 2 + core) * part_rows
        return pl.ds(pl.multiple_of(first, part_rows), part_rows)

    wx_copies = []

    def pass_on(group):
        mine = w_ref.at[:, lax.rem(y + group, n_y), row_part(0), :]
        for i in (1, n_x - 1):
            k = len(wx_copies)
            wx_copies.append(remote(mine, mine, wx_send.at[k], wx_recv.at[k], at_x(i)))
            wx_copies[-1].start()

    def take_in(distances):
        for i in distances:
            k = 2 * (1, 7, 2, 6, 3, 5, 4).index(i)
            wy_copies[k].wait_recv()
            wy_copies[k + 1].wait_recv()
            pass_on(n_y - i)

    loads[5].wait()
    loads[6].wait()
    pass_on(0)

    docs = doc_ref.shape[1]
    lens = jnp.broadcast_to(doc_ref[...].astype(F32), (docs, docs))
    sub = lax.broadcasted_iota(jnp.int32, (docs, docs), 0)
    lane = lax.broadcasted_iota(jnp.int32, (docs, docs), 1)
    lens_col = jnp.sum(jnp.where(sub == lane, lens, 0.0), axis=1, keepdims=True)
    starts = jnp.sum(jnp.where(sub < lane, lens_col, 0.0), axis=0, keepdims=True)
    row_abs = (lax.broadcasted_iota(jnp.int32, (rows, docs), 0) + c * rows).astype(F32)
    row_start = jnp.max(jnp.where(starts <= row_abs, starts, 0.0), axis=1, keepdims=True)
    row_id = lax.broadcasted_iota(jnp.int32, (rows, 1), 0)
    low = row_start - (row_id + c * rows).astype(F32) + row_id.astype(F32)
    low = jnp.maximum(low, ((row_id // BLOCK_ROWS) * BLOCK_ROWS - back).astype(F32))
    for first in range(0, win, 128):
        key_rel = (lax.broadcasted_iota(jnp.int32, (rows, 128), 1) + (first - back)).astype(F32)
        seen = (key_rel <= row_id.astype(F32)) & (key_rel >= low)
        bias_ref[:, first:first + 128] = jnp.where(seen, 0.0, NEG_BIG)

    def clear_head(h, _):
        for b in range(rows // BLOCK_ROWS):
            rows_at = pl.ds(pl.multiple_of(h * rows + b * BLOCK_ROWS, BLOCK_ROWS), BLOCK_ROWS)
            for first in range(0, win, BLOCK_ROWS):
                if first < b * BLOCK_ROWS or first >= b * BLOCK_ROWS + LONGEST_ROWS:
                    for ref in (p_ref, ds_ref):
                        ref[rows_at, first:first + BLOCK_ROWS] = jnp.zeros((BLOCK_ROWS, BLOCK_ROWS), BF16)
        return 0

    lax.fori_loop(0, heads, clear_head, 0)

    loads[2].wait()
    loads[3].wait()
    for h in range(heads):
        cols = slice(h * HEAD_SIZE, (h + 1) * HEAD_SIZE)
        qt_ref[:, h * rows:(h + 1) * rows] = q_ref[:, cols].T
        gt_ref[:, h * rows:(h + 1) * rows] = g_ref[:, cols].T

    for near, far in zip(key_copies, value_copies):
        near.wait_recv()
        far.start()
    take_in((1, 7, 2, 6))
    for copy in wy_copies[8:]:
        copy.start()

    def head_cols(h):
        return pl.ds(pl.multiple_of(h * HEAD_SIZE, HEAD_SIZE), HEAD_SIZE)

    def head_rows(h):
        return pl.ds(pl.multiple_of(h * rows, rows), rows)

    def block_of(h, b):
        rows_at = pl.ds(pl.multiple_of(h * rows + b * BLOCK_ROWS, BLOCK_ROWS), BLOCK_ROWS)
        here = slice(b * BLOCK_ROWS, (b + 1) * BLOCK_ROWS)
        return rows_at, here, slice(b * BLOCK_ROWS, b * BLOCK_ROWS + LONGEST_ROWS)

    def softmax_head(h, _):
        for b in range(rows // BLOCK_ROWS):
            rows_at, here, keys = block_of(h, b)
            s = dot_nt(q_ref[here, head_cols(h)], kwin[keys, :]) * (scale * LOG2E) + bias_ref[here, keys]
            top = jnp.max(s, axis=1, keepdims=True)
            e = jnp.exp2(s - top)
            total = jnp.sum(e, axis=1, keepdims=True)
            p_ref[rows_at, keys] = (e * (1.0 / total)).astype(BF16)
        return 0

    lax.fori_loop(0, heads, softmax_head, 0, unroll=4)

    chunks = [(0, rows - (reach * rows - back), reach)]
    chunks += [(back - i * rows, rows, i) for i in range(reach - 1, -1, -1)]

    def term_copies(kv):
        copies = []
        for first, size, i in chunks[:-1]:
            copies.append(remote(
                term_ref.at[kv, i - 1, :, pl.ds(rows - size, size)],
                inbox_ref.at[kv, i - 1, :, pl.ds(rows - size, size)],
                term_send.at[kv * reach + i - 1], term_recv.at[kv * reach + i - 1], at_ctx(-i),
            ))
        return copies

    def terms(kv, left_ref, right_ref, factor):
        copies = term_copies(kv)
        for (first, size, i), copy in zip(chunks, copies + [None]):
            part = dot_nn(left_ref[...], right_ref[:, first:first + size])
            if factor != 1.0:
                part = part * factor
            if i > 0:
                term_ref[kv, i - 1, :, rows - size:] = part.astype(BF16)
                copy.start()
            else:
                own_ref[kv] = part
        return copies

    value_terms = terms(1, gt_ref, p_ref, 1.0)

    before = w_ref.at[0, :, row_part(-1), :]
    after = w_ref.at[1, :, row_part(1), :]
    wx_far = [
        remote(before, before, wx_send.at[2 * n_y], wx_recv.at[2 * n_y], at_x(1)),
        remote(after, after, wx_send.at[2 * n_y + 1], wx_recv.at[2 * n_y + 1], at_x(n_x - 1)),
    ]
    wc_copies = []
    for k, i in enumerate((0, -1, 1, 2)):
        part = w_ref.at[:, :, row_part(i), :]
        wc_copies.append(remote(part, part, wc_send.at[k], wc_recv.at[k], (peer, y)))
    loads[4].wait()
    for copy in value_copies:
        copy.wait_recv()

    def score_head(h, _):
        grad = g_ref[:, head_cols(h)]
        delta = jnp.sum(grad.astype(F32) * o_ref[:, head_cols(h)].astype(F32), axis=1, keepdims=True)
        for b in range(rows // BLOCK_ROWS):
            rows_at, here, keys = block_of(h, b)
            dp = dot_nt(grad[here, :], vwin[keys, :])
            ds_ref[rows_at, keys] = (p_ref[rows_at, keys].astype(F32) * (dp - delta[here, :])).astype(BF16)
        return 0

    def query_head(h, _):
        for b in range(rows // BLOCK_ROWS):
            rows_at, here, keys = block_of(h, b)
            dq = dot_nn(ds_ref[rows_at, keys], kwin[keys, :]) * scale
            dq_ref[here, head_cols(h)] = dq.astype(BF16)
        return 0

    def own_sum(kv, copies):
        for copy in copies:
            copy.wait_recv()
        total = own_ref[kv]
        for i in range(1, reach):
            total = total + inbox_ref[kv, i - 1].astype(F32)
        size = chunks[0][1]
        cut = rows - size
        last = total[:, cut:] + inbox_ref[kv, reach - 1, :, cut:].astype(F32)
        slab = kv * n_y + y
        all_ref[slab, :, :cut] = total[:, :cut].astype(BF16)
        all_ref[slab, :, cut:] = last.astype(BF16)


    way = 1 - 2 * core

    def slab_at(kv, i):
        return kv * n_y + lax.rem(y + way * i + n_y, n_y)

    def gather_copies(kv):
        copies = []
        for k, (i, j) in enumerate(((0, 2), (0, -2), (0, 1), (0, -1), (-2, 1), (2, -1), (-2, 2))):
            slab = all_ref.at[slab_at(kv, i)]
            copies.append(remote(slab, slab, ay_send.at[kv * 7 + k], ay_recv.at[kv * 7 + k], at_y(way * j)))
        return copies

    def gather_first(copies):
        for copy in copies[:4]:
            copy.start()

    def gather_second(copies):
        copies[0].wait_recv()
        copies[4].start()
        copies[1].wait_recv()
        copies[5].start()
        copies[6].start()

    lax.fori_loop(0, heads, score_head, 0, unroll=4)
    key_terms = terms(0, qt_ref, ds_ref, scale)
    take_in((3, 5, 4))
    wc_copies[0].start()
    own_sum(1, value_terms)
    value_gather = gather_copies(1)
    gather_first(value_gather)
    lax.fori_loop(0, heads // 2, query_head, 0, unroll=4)
    gather_second(value_gather)
    lax.fori_loop(heads // 2, heads, query_head, 0, unroll=4)
    dq_out = pltpu.make_async_copy(dq_ref, dq_hbm, out_sem.at[0])
    dq_out.start()
    own_sum(0, key_terms)
    key_gather = gather_copies(0)
    gather_first(key_gather)
    for copy in wx_copies:
        copy.wait_recv()
    for copy in wx_far + wc_copies[1:3]:
        copy.start()
    tile = 256
    tiles = model_rows // tile

    def project(kv, t, slabs):
        row = pl.ds(pl.multiple_of(t * tile, tile), tile)
        left = jnp.concatenate([w_ref[kv, g, row, :] for g in slabs], axis=1)
        right = jnp.concatenate([all_ref[kv * n_y + g] for g in slabs], axis=0)
        return row, dot_nn(left, right)

    def project_values(t, _):
        row, part = project(1, t, range(n_y))
        acc_ref[row, :] = part
        return 0

    def project_near(t, _):
        row, part = project(0, t, [slab_at(0, i) for i in (-2, 2, 0, -1, 1)])
        acc_ref[row, :] = acc_ref[row, :] + part
        return 0

    def project_far(t, _):
        row, part = project(0, t, [slab_at(0, i) for i in (-3, 3, 4)])
        gi_ref[row, :] = (acc_ref[row, :] + part).astype(BF16)
        return 0

    gather_second(key_gather)
    for copy in wx_far:
        copy.wait_recv()
    wc_copies[3].start()
    for copy in value_gather[2:] + wc_copies:
        copy.wait_recv()
    lax.fori_loop(0, tiles, project_values, 0)
    key_gather[2].wait_recv()
    key_gather[3].wait_recv()
    lax.fori_loop(0, tiles, project_near, 0)
    for copy in key_gather[4:]:
        copy.wait_recv()
    lax.fori_loop(0, tiles, project_far, 0)
    gi_out = pltpu.make_async_copy(gi_ref, gi_hbm, out_sem.at[1])
    gi_out.start()

    for copy in key_copies + value_copies + wy_copies + wx_copies + wx_far + wc_copies + value_terms + key_terms + value_gather + key_gather:
        copy.wait_send()
    dq_out.wait()
    gi_out.wait()


def hand_over(dq_in, gi_in, dq_out, gi_out, sem):
    copies = [
        pltpu.make_async_copy(dq_in, dq_out, sem.at[0]),
        pltpu.make_async_copy(gi_in, gi_out, sem.at[1]),
    ]
    for copy in copies:
        copy.start()
    for copy in copies:
        copy.wait()


def body(n_ctx, n_y, n_x, q, k, v, o, g, kp, vp, doc_lengths):
    rows, width = q.shape
    heads = width // HEAD_SIZE
    model_rows = kp.shape[0] // n_y
    reach = LONGEST_ROWS // rows
    win = LONGEST_ROWS - BLOCK_ROWS + rows
    hops = n_y - 1
    dma = pltpu.SemaphoreType.DMA
    any_spec = pl.BlockSpec(memory_space=pl.ANY)
    dq, gi = pl.pallas_call(
        functools.partial(kernel, n_ctx, n_y, n_x),
        out_shape=(
            jax.ShapeDtypeStruct((rows, width), BF16),
            jax.ShapeDtypeStruct((model_rows, rows), BF16),
        ),
        in_specs=[any_spec] * 7 + [pl.BlockSpec(memory_space=pltpu.VMEM)],
        out_specs=(any_spec, any_spec),
        scratch_shapes=[
            pltpu.VMEM((rows, width), BF16),
            pltpu.VMEM((rows, width), BF16),
            pltpu.VMEM((rows, width), BF16),
            pltpu.VMEM((HEAD_SIZE, heads * rows), BF16),
            pltpu.VMEM((HEAD_SIZE, heads * rows), BF16),
            pltpu.VMEM((win, HEAD_SIZE), BF16),
            pltpu.VMEM((win, HEAD_SIZE), BF16),
            pltpu.VMEM((rows, win), F32),
            pltpu.VMEM((heads * rows, win), BF16),
            pltpu.VMEM((heads * rows, win), BF16),
            pltpu.VMEM((2, n_y, model_rows, HEAD_SIZE), BF16),
            pltpu.VMEM((2 * n_y, HEAD_SIZE, rows), BF16),
            pltpu.VMEM((2, reach, HEAD_SIZE, rows), BF16),
            pltpu.VMEM((2, reach, HEAD_SIZE, rows), BF16),
            pltpu.VMEM((2, HEAD_SIZE, rows), F32),
            pltpu.VMEM((model_rows, rows), F32),
            pltpu.VMEM((rows, width), BF16),
            pltpu.VMEM((model_rows, rows), BF16),
            dma((7,)), dma((2,)),
            dma((2 * reach,)), dma((2 * reach,)),
            dma((2 * reach,)), dma((2 * reach,)),
            dma((2 * hops,)), dma((2 * hops,)),
            dma((2 * n_y + 2,)), dma((2 * n_y + 2,)),
            dma((n_x,)), dma((n_x,)),
            dma((14,)), dma((14,)),
        ],
        compiler_params=pltpu.CompilerParams(
            collective_id=0, has_side_effects=True, vmem_limit_bytes=56 * 1024 * 1024
        ),
    )(q, k, v, o, g, kp, vp, doc_lengths.reshape(1, -1))
    return pl.pallas_call(
        hand_over,
        out_shape=(
            jax.ShapeDtypeStruct(dq.shape, BF16),
            jax.ShapeDtypeStruct(gi.shape, BF16),
        ),
        in_specs=[pl.BlockSpec(memory_space=pltpu.VMEM)] * 2,
        out_specs=(any_spec, any_spec),
        scratch_shapes=[dma((2,))],
    )(dq, gi)


def build(mesh, n_x):
    return jax.shard_map(
        functools.partial(body, mesh.shape["ctx"], mesh.shape["head"], n_x),
        mesh=mesh,
        in_specs=(
            P("ctx", "head"),
            P("ctx", "head"),
            P("ctx", "head"),
            P("ctx", "head"),
            P("ctx", "head"),
            P(None, "head"),
            P(None, "head"),
            P(),
        ),
        out_specs=(P("ctx", "head"), P("head", "ctx")),
        check_vma=False,
    )


def solution(mesh):
    return build(mesh, X_CHIPS)
```

```python
import functools

import jax
import jax.numpy as jnp
from jax import lax
from jax.experimental import pallas as pl
from jax.experimental.pallas import tpu as pltpu
from jax.sharding import PartitionSpec as P

MESH = pl.DeviceIdType.MESH
HEAD_SIZE = 128
BLOCK_ROWS = 128
LONGEST_ROWS = 1024
X_CHIPS = 4
NEG_BIG = -1.0e30
LOG2E = 1.4426950408889634

F32 = jnp.float32
BF16 = jnp.bfloat16


def dot_nn(a, b):
    return lax.dot_general(a, b, (((1,), (0,)), ((), ())), preferred_element_type=F32)


def dot_nt(a, b):
    return lax.dot_general(a, b, (((1,), (1,)), ((), ())), preferred_element_type=F32)


def kernel(
    n_ctx, n_y, n_x,
    q_hbm, k_hbm, v_hbm, o_hbm, g_hbm, kp_hbm, vp_hbm, doc_ref,
    dq_hbm, gi_hbm,
    q_ref, g_ref, o_ref, qt_ref, gt_ref, kwin, vwin, bias_ref, p_ref, ds_ref,
    w_ref, all_ref, term_ref, inbox_ref, own_ref, acc_ref, dq_ref, gi_ref,
    load_sem, out_sem, ctx_send, ctx_recv, term_send, term_recv,
    wy_send, wy_recv, wx_send, wx_recv, wc_send, wc_recv, ay_send, ay_recv,
):
    rows, width = q_hbm.shape
    heads = width // HEAD_SIZE
    back = LONGEST_ROWS - BLOCK_ROWS
    win = back + rows
    reach = LONGEST_ROWS // rows
    model_rows = gi_hbm.shape[0]
    part_rows = model_rows // (2 * n_x)
    scale = HEAD_SIZE ** -0.5

    c = lax.axis_index("ctx")
    y = lax.axis_index("head")
    per_x = n_ctx // n_x
    x = c // per_x
    inner = c % per_x
    core = c % 2
    peer = c + 1 - 2 * core

    def at_ctx(i):
        return (lax.rem(c + i + n_ctx, n_ctx), y)

    def at_y(i):
        return (c, lax.rem(y + i + n_y, n_y))

    def at_x(i):
        return (lax.rem(x + i, n_x) * per_x + inner, y)

    def remote(src, dst, send, recv, to):
        return pltpu.make_async_remote_copy(
            src_ref=src, dst_ref=dst, send_sem=send, recv_sem=recv, device_id=to, device_id_type=MESH
        )

    loads = [
        pltpu.make_async_copy(k_hbm, kwin.at[pl.ds(back, rows), :], load_sem.at[0]),
        pltpu.make_async_copy(v_hbm, vwin.at[pl.ds(back, rows), :], load_sem.at[1]),
        pltpu.make_async_copy(q_hbm, q_ref, load_sem.at[2]),
        pltpu.make_async_copy(g_hbm, g_ref, load_sem.at[3]),
        pltpu.make_async_copy(o_hbm, o_ref, load_sem.at[4]),
    ]
    my_part = pl.multiple_of((x * 2 + core) * part_rows, part_rows)
    my_rows = pl.multiple_of(y * model_rows + my_part, part_rows)
    for kv, src in ((0, kp_hbm), (1, vp_hbm)):
        loads.append(pltpu.make_async_copy(
            src.at[pl.ds(my_rows, part_rows), :],
            w_ref.at[kv, y, pl.ds(my_part, part_rows), :],
            load_sem.at[5 + kv],
        ))
    for copy in loads:
        copy.start()

    loads[0].wait()
    loads[1].wait()
    barrier = pltpu.get_barrier_semaphore()
    partners = [at_ctx(i) for i in range(-reach, reach + 1) if i != 0]
    partners += [at_y(i) for i in range(1, n_y)] + [at_x(i) for i in range(1, n_x)]
    for to in partners:
        pl.semaphore_signal(barrier, inc=1, device_id=to, device_id_type=MESH)
    pl.semaphore_wait(barrier, len(partners))

    def context_copies(kv, ref):
        copies = []
        for i in range(1, reach + 1):
            first = max(back - i * rows, 0)
            cut = max(i * rows - back, 0)
            copies.append(remote(
                ref.at[pl.ds(back + cut, rows - cut), :], ref.at[pl.ds(first, rows - cut), :],
                ctx_send.at[kv * reach + i - 1], ctx_recv.at[kv * reach + i - 1], at_ctx(i),
            ))
        return copies

    key_copies = context_copies(0, kwin)
    value_copies = context_copies(1, vwin)
    for copy in key_copies:
        copy.start()

    wy_copies = []
    for i in (1, 7, 2, 6, 3, 5, 4):
        other = lax.rem(y + i, n_y)
        theirs = pl.multiple_of(other * model_rows + my_part, part_rows)
        for kv, src in ((0, kp_hbm), (1, vp_hbm)):
            wy_copies.append(remote(
                src.at[pl.ds(theirs, part_rows), :],
                w_ref.at[kv, y, pl.ds(my_part, part_rows), :],
                wy_send.at[2 * (i - 1) + kv], wy_recv.at[2 * (i - 1) + kv], at_y(i),
            ))
    for copy in wy_copies[:8]:
        copy.start()

    def row_part(i):
        first = (lax.rem(x + i + n_x, n_x) * 2 + core) * part_rows
        return pl.ds(pl.multiple_of(first, part_rows), part_rows)

    wx_copies = []

    def pass_on(group):
        mine = w_ref.at[:, lax.rem(y + group, n_y), row_part(0), :]
        for i in (1, n_x - 1):
            k = len(wx_copies)
            wx_copies.append(remote(mine, mine, wx_send.at[k], wx_recv.at[k], at_x(i)))
            wx_copies[-1].start()

    def take_in(distances):
        for i in distances:
            k = 2 * (1, 7, 2, 6, 3, 5, 4).index(i)
            wy_copies[k].wait_recv()
            wy_copies[k + 1].wait_recv()
            pass_on(n_y - i)

    loads[5].wait()
    loads[6].wait()
    pass_on(0)

    docs = doc_ref.shape[1]
    lens = jnp.broadcast_to(doc_ref[...].astype(F32), (docs, docs))
    sub = lax.broadcasted_iota(jnp.int32, (docs, docs), 0)
    lane = lax.broadcasted_iota(jnp.int32, (docs, docs), 1)
    lens_col = jnp.sum(jnp.where(sub == lane, lens, 0.0), axis=1, keepdims=True)
    starts = jnp.sum(jnp.where(sub < lane, lens_col, 0.0), axis=0, keepdims=True)
    row_abs = (lax.broadcasted_iota(jnp.int32, (rows, docs), 0) + c * rows).astype(F32)
    row_start = jnp.max(jnp.where(starts <= row_abs, starts, 0.0), axis=1, keepdims=True)
    row_id = lax.broadcasted_iota(jnp.int32, (rows, 1), 0)
    low = row_start - (row_id + c * rows).astype(F32) + row_id.astype(F32)
    low = jnp.maximum(low, ((row_id // BLOCK_ROWS) * BLOCK_ROWS - back).astype(F32))
    for first in range(0, win, 128):
        key_rel = (lax.broadcasted_iota(jnp.int32, (rows, 128), 1) + (first - back)).astype(F32)
        seen = (key_rel <= row_id.astype(F32)) & (key_rel >= low)
        bias_ref[:, first:first + 128] = jnp.where(seen, 0.0, NEG_BIG)

    def clear_head(h, _):
        for b in range(rows // BLOCK_ROWS):
            rows_at = pl.ds(pl.multiple_of(h * rows + b * BLOCK_ROWS, BLOCK_ROWS), BLOCK_ROWS)
            for first in range(0, win, BLOCK_ROWS):
                if first < b * BLOCK_ROWS or first >= b * BLOCK_ROWS + LONGEST_ROWS:
                    for ref in (p_ref, ds_ref):
                        ref[rows_at, first:first + BLOCK_ROWS] = jnp.zeros((BLOCK_ROWS, BLOCK_ROWS), BF16)
        return 0

    lax.fori_loop(0, heads, clear_head, 0)

    loads[2].wait()
    loads[3].wait()
    for h in range(heads):
        cols = slice(h * HEAD_SIZE, (h + 1) * HEAD_SIZE)
        qt_ref[:, h * rows:(h + 1) * rows] = q_ref[:, cols].T
        gt_ref[:, h * rows:(h + 1) * rows] = g_ref[:, cols].T

    take_in((1, 7, 2, 6))
    for copy in wy_copies[8:]:
        copy.start()
    for near, far in zip(key_copies, value_copies):
        near.wait_recv()
        far.start()

    def head_cols(h):
        return pl.ds(pl.multiple_of(h * HEAD_SIZE, HEAD_SIZE), HEAD_SIZE)

    def head_rows(h):
        return pl.ds(pl.multiple_of(h * rows, rows), rows)

    def block_of(h, b):
        rows_at = pl.ds(pl.multiple_of(h * rows + b * BLOCK_ROWS, BLOCK_ROWS), BLOCK_ROWS)
        here = slice(b * BLOCK_ROWS, (b + 1) * BLOCK_ROWS)
        return rows_at, here, slice(b * BLOCK_ROWS, b * BLOCK_ROWS + LONGEST_ROWS)

    def softmax_head(h, _):
        for b in range(rows // BLOCK_ROWS):
            rows_at, here, keys = block_of(h, b)
            s = dot_nt(q_ref[here, head_cols(h)], kwin[keys, :]) * (scale * LOG2E) + bias_ref[here, keys]
            top = jnp.max(s, axis=1, keepdims=True)
            e = jnp.exp2(s - top)
            total = jnp.sum(e, axis=1, keepdims=True)
            p_ref[rows_at, keys] = (e * (1.0 / total)).astype(BF16)
        return 0

    lax.fori_loop(0, heads, softmax_head, 0, unroll=4)

    chunks = [(0, rows - (reach * rows - back), reach)]
    chunks += [(back - i * rows, rows, i) for i in range(reach - 1, -1, -1)]

    def term_copies(kv):
        copies = []
        for first, size, i in chunks[:-1]:
            copies.append(remote(
                term_ref.at[kv, i - 1, :, pl.ds(rows - size, size)],
                inbox_ref.at[kv, i - 1, :, pl.ds(rows - size, size)],
                term_send.at[kv * reach + i - 1], term_recv.at[kv * reach + i - 1], at_ctx(-i),
            ))
        return copies

    def terms(kv, left_ref, right_ref, factor):
        copies = term_copies(kv)
        for (first, size, i), copy in zip(chunks, copies + [None]):
            part = dot_nn(left_ref[...], right_ref[:, first:first + size])
            if factor != 1.0:
                part = part * factor
            if i > 0:
                term_ref[kv, i - 1, :, rows - size:] = part.astype(BF16)
                copy.start()
            else:
                own_ref[kv] = part
        return copies

    value_terms = terms(1, gt_ref, p_ref, 1.0)

    before = w_ref.at[0, :, row_part(-1), :]
    after = w_ref.at[1, :, row_part(1), :]
    wx_far = [
        remote(before, before, wx_send.at[2 * n_y], wx_recv.at[2 * n_y], at_x(1)),
        remote(after, after, wx_send.at[2 * n_y + 1], wx_recv.at[2 * n_y + 1], at_x(n_x - 1)),
    ]
    wc_copies = []
    for k, i in enumerate((0, -1, 1, 2)):
        part = w_ref.at[:, :, row_part(i), :]
        wc_copies.append(remote(part, part, wc_send.at[k], wc_recv.at[k], (peer, y)))
    loads[4].wait()
    for copy in value_copies:
        copy.wait_recv()

    def score_head(h, _):
        grad = g_ref[:, head_cols(h)]
        delta = jnp.sum(grad.astype(F32) * o_ref[:, head_cols(h)].astype(F32), axis=1, keepdims=True)
        for b in range(rows // BLOCK_ROWS):
            rows_at, here, keys = block_of(h, b)
            dp = dot_nt(grad[here, :], vwin[keys, :])
            ds_ref[rows_at, keys] = (p_ref[rows_at, keys].astype(F32) * (dp - delta[here, :])).astype(BF16)
        return 0

    def query_head(h, _):
        for b in range(rows // BLOCK_ROWS):
            rows_at, here, keys = block_of(h, b)
            dq = dot_nn(ds_ref[rows_at, keys], kwin[keys, :]) * scale
            dq_ref[here, head_cols(h)] = dq.astype(BF16)
        return 0

    def own_sum(kv, copies):
        for copy in copies:
            copy.wait_recv()
        total = own_ref[kv]
        for i in range(1, reach):
            total = total + inbox_ref[kv, i - 1].astype(F32)
        size = chunks[0][1]
        cut = rows - size
        last = total[:, cut:] + inbox_ref[kv, reach - 1, :, cut:].astype(F32)
        slab = kv * n_y + y
        all_ref[slab, :, :cut] = total[:, :cut].astype(BF16)
        all_ref[slab, :, cut:] = last.astype(BF16)


    way = 1 - 2 * core

    def slab_at(kv, i):
        return kv * n_y + lax.rem(y + way * i + n_y, n_y)

    def gather_copies(kv):
        copies = []
        for k, (i, j) in enumerate(((0, 2), (0, -2), (0, 1), (0, -1), (-2, 1), (2, -1), (-2, 2))):
            slab = all_ref.at[slab_at(kv, i)]
            copies.append(remote(slab, slab, ay_send.at[kv * 7 + k], ay_recv.at[kv * 7 + k], at_y(way * j)))
        return copies

    def gather_first(copies):
        for copy in copies[:4]:
            copy.start()

    def gather_second(copies):
        copies[0].wait_recv()
        copies[4].start()
        copies[1].wait_recv()
        copies[5].start()
        copies[6].start()

    lax.fori_loop(0, heads, score_head, 0, unroll=4)
    take_in((3, 5, 4))
    wc_copies[0].start()
    key_terms = terms(0, qt_ref, ds_ref, scale)
    own_sum(1, value_terms)
    value_gather = gather_copies(1)
    gather_first(value_gather)
    lax.fori_loop(0, heads // 2, query_head, 0, unroll=4)
    gather_second(value_gather)
    lax.fori_loop(heads // 2, heads, query_head, 0, unroll=4)
    dq_out = pltpu.make_async_copy(dq_ref, dq_hbm, out_sem.at[0])
    dq_out.start()
    for copy in wx_copies:
        copy.wait_recv()
    for copy in wx_far + wc_copies[1:3]:
        copy.start()
    own_sum(0, key_terms)
    key_gather = gather_copies(0)
    gather_first(key_gather)
    tile = 2 * part_rows
    tiles = n_x

    def project(kv, t, slabs):
        row = pl.ds(pl.multiple_of(t * tile, tile), tile)
        left = jnp.concatenate([w_ref[kv, g, row, :] for g in slabs], axis=1)
        right = jnp.concatenate([all_ref[kv * n_y + g] for g in slabs], axis=0)
        return row, dot_nn(left, right)

    def project_values(t, _):
        row, part = project(1, t, range(n_y))
        acc_ref[row, :] = part
        return 0

    def project_near(t, _):
        row, part = project(0, t, [slab_at(0, i) for i in (-2, 2, 0, -1, 1)])
        acc_ref[row, :] = acc_ref[row, :] + part
        return 0

    def project_far(t, _):
        row, part = project(0, t, [slab_at(0, i) for i in (-3, 3, 4)])
        gi_ref[row, :] = (acc_ref[row, :] + part).astype(BF16)
        return 0

    def tiles_of(parts, step):
        for i in parts:
            step(lax.rem(x + i + n_x, n_x), 0)

    gather_second(key_gather)
    for copy in value_gather[2:] + wc_copies[:3]:
        copy.wait_recv()
    tiles_of((0, -1, 1), project_values)
    for copy in wx_far:
        copy.wait_recv()
    wc_copies[3].start()
    key_gather[2].wait_recv()
    key_gather[3].wait_recv()
    tiles_of((0, -1, 1), project_near)
    wc_copies[3].wait_recv()
    tiles_of((2,), project_values)
    tiles_of((2,), project_near)
    for copy in key_gather[4:]:
        copy.wait_recv()
    lax.fori_loop(0, tiles, project_far, 0)
    gi_out = pltpu.make_async_copy(gi_ref, gi_hbm, out_sem.at[1])
    gi_out.start()

    for copy in key_copies + value_copies + wy_copies + wx_copies + wx_far + wc_copies + value_terms + key_terms + value_gather + key_gather:
        copy.wait_send()
    dq_out.wait()
    gi_out.wait()


def hand_over(dq_in, gi_in, dq_out, gi_out, sem):
    copies = [
        pltpu.make_async_copy(dq_in, dq_out, sem.at[0]),
        pltpu.make_async_copy(gi_in, gi_out, sem.at[1]),
    ]
    for copy in copies:
        copy.start()
    for copy in copies:
        copy.wait()


def body(n_ctx, n_y, n_x, q, k, v, o, g, kp, vp, doc_lengths):
    rows, width = q.shape
    heads = width // HEAD_SIZE
    model_rows = kp.shape[0] // n_y
    reach = LONGEST_ROWS // rows
    win = LONGEST_ROWS - BLOCK_ROWS + rows
    hops = n_y - 1
    dma = pltpu.SemaphoreType.DMA
    any_spec = pl.BlockSpec(memory_space=pl.ANY)
    dq, gi = pl.pallas_call(
        functools.partial(kernel, n_ctx, n_y, n_x),
        out_shape=(
            jax.ShapeDtypeStruct((rows, width), BF16),
            jax.ShapeDtypeStruct((model_rows, rows), BF16),
        ),
        in_specs=[any_spec] * 7 + [pl.BlockSpec(memory_space=pltpu.VMEM)],
        out_specs=(any_spec, any_spec),
        scratch_shapes=[
            pltpu.VMEM((rows, width), BF16),
            pltpu.VMEM((rows, width), BF16),
            pltpu.VMEM((rows, width), BF16),
            pltpu.VMEM((HEAD_SIZE, heads * rows), BF16),
            pltpu.VMEM((HEAD_SIZE, heads * rows), BF16),
            pltpu.VMEM((win, HEAD_SIZE), BF16),
            pltpu.VMEM((win, HEAD_SIZE), BF16),
            pltpu.VMEM((rows, win), F32),
            pltpu.VMEM((heads * rows, win), BF16),
            pltpu.VMEM((heads * rows, win), BF16),
            pltpu.VMEM((2, n_y, model_rows, HEAD_SIZE), BF16),
            pltpu.VMEM((2 * n_y, HEAD_SIZE, rows), BF16),
            pltpu.VMEM((2, reach, HEAD_SIZE, rows), BF16),
            pltpu.VMEM((2, reach, HEAD_SIZE, rows), BF16),
            pltpu.VMEM((2, HEAD_SIZE, rows), F32),
            pltpu.VMEM((model_rows, rows), F32),
            pltpu.VMEM((rows, width), BF16),
            pltpu.VMEM((model_rows, rows), BF16),
            dma((7,)), dma((2,)),
            dma((2 * reach,)), dma((2 * reach,)),
            dma((2 * reach,)), dma((2 * reach,)),
            dma((2 * hops,)), dma((2 * hops,)),
            dma((2 * n_y + 2,)), dma((2 * n_y + 2,)),
            dma((n_x,)), dma((n_x,)),
            dma((14,)), dma((14,)),
        ],
        compiler_params=pltpu.CompilerParams(
            collective_id=0, has_side_effects=True, vmem_limit_bytes=56 * 1024 * 1024
        ),
    )(q, k, v, o, g, kp, vp, doc_lengths.reshape(1, -1))
    return pl.pallas_call(
        hand_over,
        out_shape=(
            jax.ShapeDtypeStruct(dq.shape, BF16),
            jax.ShapeDtypeStruct(gi.shape, BF16),
        ),
        in_specs=[pl.BlockSpec(memory_space=pltpu.VMEM)] * 2,
        out_specs=(any_spec, any_spec),
        scratch_shapes=[dma((2,))],
    )(dq, gi)


def build(mesh, n_x):
    return jax.shard_map(
        functools.partial(body, mesh.shape["ctx"], mesh.shape["head"], n_x),
        mesh=mesh,
        in_specs=(
            P("ctx", "head"),
            P("ctx", "head"),
            P("ctx", "head"),
            P("ctx", "head"),
            P("ctx", "head"),
            P(None, "head"),
            P(None, "head"),
            P(),
        ),
        out_specs=(P("ctx", "head"), P("head", "ctx")),
        check_vma=False,
    )


def solution(mesh):
    return build(mesh, X_CHIPS)
```
